32 devices in a mesh: group: 4 (over y, x), mp: 8 (over z, core).
Axes of the slice: x: 2, y: 2, z: 4, core: 2. Of those that a mesh axis runs over, the one named last changes fastest.
Arguments:
- tokens: bfloat16 [640, 4096], P(None, 'group'), may hold values from -6 to 6
- trunk_gate: bfloat16 [4096, 11008], P('group', 'mp'), may hold values from -0.09375 to 0.09375
- trunk_up: bfloat16 [4096, 11008], P('group', 'mp'), may hold values from -0.09375 to 0.09375
- trunk_down: bfloat16 [11008, 4096], P('mp', 'group'), may hold values from -0.0546875 to 0.0546875
- head_gate: bfloat16 [4, 4096, 11008], P('group', None, 'mp'), may hold values from -0.09375 to 0.09375
- head_up: bfloat16 [4, 4096, 11008], P('group', None, 'mp'), may hold values from -0.09375 to 0.09375
- head_down: bfloat16 [4, 11008, 4096], P('group', 'mp'), may hold values from -0.0546875 to 0.0546875
- head_grads: bfloat16 [4, 640, 4096], P('group', None, 'mp'), may hold values from -6 to 6
Outputs:
- grad_x: bfloat16 [640, 4096], P('mp', 'group')
- grad_gate: float32 [4096, 11008], P('group', 'mp')
- grad_up: float32 [4096, 11008], P('group', 'mp')
- grad_down: float32 [11008, 4096], P('mp', 'group')
The draws below stay inside these ranges and needn't reach their ends.
All inputs are finite; a program needn't handle non-finite values.
Results may differ from the reference program's by a relative error of at most 0.009.
Values may be sent and summed in bfloat16 or wider, within the bound.
No kernel may reach another device: no remote copies, remote signals or barrier semaphores. Data moves between devices by JAX's collectives and lax.ppermute only.
A program may use at most 192 MiB of HBM per device.

```python
import jax
import jax.numpy as jnp
from jax import lax

D = 4096
FF = 11008
TOKENS = 640
HEADS = 4


def levels(stream_key, shape, shards, smallest, largest):
    level, own = 1.0, jax.random.fold_in(stream_key, 6)
    for position, parts in shards:
        heights = jnp.exp(jax.random.uniform(jax.random.fold_in(own, position), (parts,), jnp.float32, smallest / len(shards), largest / len(shards)))
        level = level * jnp.repeat(heights, shape[position] // parts).reshape([-1 if axis == position else 1 for axis in range(len(shape))])
    return level


def scatter_about(rng, shape, spread, limit, shards=(), kind=jnp.bfloat16):
    level = levels(rng, shape, shards, -0.22, 0.18) if shards else 1.0
    drawn = jax.random.normal(rng, shape, jnp.float32) * spread * level
    return jnp.minimum(jnp.maximum(drawn, -limit), limit).astype(kind)


def setup_inputs(seed: int = 0) -> dict:
    key_list = jax.random.split(jax.random.key(seed), 9)
    tokens = scatter_about(key_list[0], (TOKENS, D), 1.0, 6.0, ((1, 4),))
    trunk_gate = scatter_about(key_list[1], (D, FF), D ** -0.5, 0.09375, ((0, 4), (1, 8)))
    trunk_up = scatter_about(key_list[2], (D, FF), D ** -0.5, 0.09375, ((0, 4), (1, 8)))
    trunk_down = scatter_about(key_list[3], (FF, D), FF ** -0.5, 0.0546875, ((0, 8), (1, 4)))
    head_gate = scatter_about(key_list[4], (HEADS, D, FF), D ** -0.5, 0.09375, ((0, 4), (2, 8)))
    head_up = scatter_about(key_list[5], (HEADS, D, FF), D ** -0.5, 0.09375, ((0, 4), (2, 8)))
    head_down = scatter_about(key_list[6], (HEADS, FF, D), FF ** -0.5, 0.0546875, ((0, 4), (1, 8)))
    head_grads = scatter_about(key_list[7], (HEADS, TOKENS, D), 1.0, 6.0, ((0, 4), (2, 8)))
    return {"tokens": tokens, "trunk_gate": trunk_gate, "trunk_up": trunk_up, "trunk_down": trunk_down, "head_gate": head_gate, "head_up": head_up, "head_down": head_down, "head_grads": head_grads}


def silu_grad(pre_act):
    sig = jax.nn.sigmoid(pre_act)
    return sig * (1.0 + pre_act * (1.0 - sig))

def contract_last(left, right):
    return lax.dot_general(left, right, (((1,), (1,)), ((), ())), preferred_element_type=jnp.float32)

def contract_first(left, right):
    return lax.dot_general(left, right, (((0,), (0,)), ((), ())), preferred_element_type=jnp.float32)

def reference(tokens, trunk_gate, trunk_up, trunk_down, head_gate, head_up, head_down, head_grads):
    gate_t = jnp.dot(tokens, trunk_gate, preferred_element_type=jnp.float32)
    up_t = jnp.dot(tokens, trunk_up, preferred_element_type=jnp.float32)
    hidden_t = (jax.nn.silu(gate_t) * up_t).astype(jnp.bfloat16)
    trunk_out = (tokens.astype(jnp.float32) + jnp.dot(hidden_t, trunk_down, preferred_element_type=jnp.float32)).astype(jnp.bfloat16)

    def one_head(running, head_item):
        gate_mat, up_mat, down_mat, cot_full = head_item
        head_pre = jnp.dot(trunk_out, gate_mat, preferred_element_type=jnp.float32)
        head_lin = jnp.dot(trunk_out, up_mat, preferred_element_type=jnp.float32)
        grad_hid = contract_last(cot_full, down_mat)
        gate_grad = (grad_hid * head_lin * silu_grad(head_pre)).astype(jnp.bfloat16)
        lin_grad = (grad_hid * jax.nn.silu(head_pre)).astype(jnp.bfloat16)
        term = cot_full.astype(jnp.float32) + contract_last(gate_grad, gate_mat) + contract_last(lin_grad, up_mat)
        return (running + term, None)
    start_sum = jnp.zeros((tokens.shape[0], tokens.shape[1]), jnp.float32)
    summed, _ = lax.scan(one_head, start_sum, (head_gate, head_up, head_down, head_grads))
    dtrunk = summed.astype(jnp.bfloat16)
    ghid_t = contract_last(dtrunk, trunk_down)
    dgate_t = (ghid_t * up_t * silu_grad(gate_t)).astype(jnp.bfloat16)
    dup_t = (ghid_t * jax.nn.silu(gate_t)).astype(jnp.bfloat16)
    grad_gate = contract_first(tokens, dgate_t)
    grad_up = contract_first(tokens, dup_t)
    grad_down = contract_first(hidden_t, dtrunk)
    grad_x = (dtrunk.astype(jnp.float32) + contract_last(dgate_t, trunk_gate) + contract_last(dup_t, trunk_up)).astype(jnp.bfloat16)
    return (grad_x, grad_gate, grad_up, grad_down)
```

```python
import functools

import jax
import jax.numpy as jnp
from jax import lax
from jax.experimental import pallas as pl
from jax.experimental.pallas import tpu as pltpu
from jax.sharding import PartitionSpec as P

BF = jnp.bfloat16
F32 = jnp.float32
MIB = 1 << 20


def silu_grad(pre_act):
    sig = jax.nn.sigmoid(pre_act)
    return sig * (1.0 + pre_act * (1.0 - sig))


def dot(left, right, dims):
    return lax.dot_general(left, right, (dims, ((), ())), preferred_element_type=F32)


def dot_nt(left, right):
    return dot(left, right, ((1,), (1,)))


def dot_nn(left, right):
    return dot(left, right, ((1,), (0,)))


def row(stack, index):
    return lax.dynamic_index_in_dim(stack, index, 0, keepdims=False)


def whole(shape):
    return pl.BlockSpec(shape, lambda *_: (0,) * len(shape))


def call(kernel, name, grid, index, in_specs, out_specs, out_shape, operands, flops, vmem, scratch=()):
    moved = sum(o.size * o.dtype.itemsize for o in operands)
    return pl.pallas_call(
        kernel,
        grid_spec=pltpu.PrefetchScalarGridSpec(
            num_scalar_prefetch=1, grid=grid, in_specs=in_specs, out_specs=out_specs, scratch_shapes=scratch
        ),
        out_shape=out_shape,
        name=name,
        cost_estimate=pl.CostEstimate(flops=flops, bytes_accessed=moved, transcendentals=0),
        compiler_params=pltpu.CompilerParams(vmem_limit_bytes=vmem * MIB),
    )(index, *operands)


class Plan:
    def __init__(self, mesh):
        self.groups = mesh.shape["group"]
        self.members = mesh.shape["mp"]
        self.places = self.members // 2

    def group_swap(self, value, mask):
        return lax.ppermute(value, "group", [(i, i ^ mask) for i in range(self.groups)])

    def core_swap(self, value):
        return lax.ppermute(value, "mp", [(i, i ^ 1) for i in range(self.members)])

    def place_swap(self, value, mask):
        return lax.ppermute(value, "mp", [(i, i ^ (2 * mask)) for i in range(self.members)])

    def gather(self, pair):
        have = {0: pair}
        if self.groups == 4:
            have[1] = self.group_swap(pair, 1)
            have[2] = self.group_swap(pair, 2)
            have[3] = (self.group_swap(have[2][0], 1), self.group_swap(have[1][1], 2))
        else:
            for k in range(1, self.groups):
                have[k] = self.group_swap(pair, k)
        return have

    def scatter(self, parts):
        if self.groups == 4:
            first = self.group_swap(parts[3][0].astype(BF), 1)
            second = self.group_swap(parts[3][1].astype(BF), 2)
            to_x = jnp.stack([parts[1][0].astype(F32), parts[1][1].astype(F32) + second.astype(F32)])
            to_y = jnp.stack([parts[2][0].astype(F32) + first.astype(F32), parts[2][1].astype(F32)])
            came_x = self.group_swap(to_x.astype(BF), 1)
            came_y = self.group_swap(to_y.astype(BF), 2)
            return parts[0].astype(F32) + (came_x.astype(F32) + came_y.astype(F32))
        total = parts[0].astype(F32)
        for k in range(1, self.groups):
            total = total + self.group_swap(parts[k].astype(BF), k).astype(F32)
        return total

    def halving(self, keep, send, first):
        current = keep.astype(F32) + self.group_swap(send, first).astype(F32)
        keys = [k for k in range(self.groups) if not k & first]
        current = {k: current[i] for i, k in enumerate(keys)}
        mask = 1
        while mask < self.groups:
            if mask != first:
                keys = [k for k in current if not k & mask]
                came = self.group_swap(jnp.stack([current[k | mask] for k in keys]).astype(BF), mask)
                current = {k: current[k] + came[i].astype(F32) for i, k in enumerate(keys)}
            mask *= 2
        return current[0]

    def place_sum(self, parts, me):
        total = row(parts, me).astype(F32)
        for mask in range(1, self.places):
            total = total + self.place_swap(row(parts, me ^ mask).astype(BF), mask).astype(F32)
        return total

    def place_gather(self, piece, me):
        out = jnp.zeros((self.places,) + piece.shape, piece.dtype)
        out = lax.dynamic_update_index_in_dim(out, piece, me, 0)
        for mask in range(1, self.places):
            out = lax.dynamic_update_index_in_dim(out, self.place_swap(piece, mask), me ^ mask, 0)
        return out


def chunks_kernel(order, index, *refs):
    n = len(order)
    value = jnp.concatenate([refs[k][...] for k in order], 0)
    product = dot_nt(value, refs[n][...])
    first, second = refs[n + 1], refs[n + 2]
    half = product.shape[0] // 2
    first[...] = product[:half].astype(BF)
    second[...] = product[half:].astype(BF)


def chunks_product(index, value, weight_t, order, name):
    n = len(order)
    rows, depth = value.shape
    units = weight_t.shape[0]
    share = rows // n
    specs = [pl.BlockSpec((share, depth), lambda i, index, k=k: (index[k], 0)) for k in range(n)]
    shape = (rows // 2, units)
    first, second = call(
        functools.partial(chunks_kernel, order),
        name,
        (1,),
        index,
        specs + [whole(weight_t.shape)],
        [whole(shape)] * 2,
        [jax.ShapeDtypeStruct(shape, BF)] * 2,
        [value] * n + [weight_t],
        2 * rows * depth * units,
        32,
    )
    return first.reshape(n // 2, share, units), second.reshape(n // 2, share, units)


def ghid_kernel(index, cot, weight, out):
    product = dot_nt(cot[0], weight[...])

    @pl.when(pl.program_id(0) == 0)
    def _():
        out[...] = product

    @pl.when(pl.program_id(0) > 0)
    def _():
        out[...] += product


def ghid_product(index, cot, weight):
    parts, rows, depth = cot.shape
    units = weight.shape[0]
    return call(
        ghid_kernel,
        "head_hidden_grad",
        (parts,),
        index,
        [
            pl.BlockSpec((1, rows, depth), lambda i, index: (i, 0, 0)),
            pl.BlockSpec((units, depth), lambda i, index: (0, i)),
        ],
        whole((rows, units)),
        jax.ShapeDtypeStruct((rows, units), F32),
        [cot, weight],
        2 * rows * units * depth * parts,
        40,
    )


def pre_kernel(n, index, *refs):
    pieces, (gate_w, up_w, pre, lin) = refs[:n], refs[n:]
    per = 2
    for j in range(n // per):

        @pl.when(pl.program_id(0) == j)
        def _(j=j):
            value = jnp.concatenate([p[...] for p in pieces[per * j : per * j + per]], 0)
            a, b = dot_nt(value, gate_w[...]), dot_nt(value, up_w[...])
            if j == 0:
                pre[...] = a
                lin[...] = b
            else:
                pre[...] += a
                lin[...] += b


def pre_product(index, pieces, gate_t, up_t):
    flat = [piece for k in range(len(pieces)) for piece in pieces[k]]
    half, depth = flat[0].shape
    units = gate_t.shape[0]
    weight = pl.BlockSpec((units, depth), lambda i, index: (0, index[i]))
    shape = jax.ShapeDtypeStruct((2 * half, units), F32)
    return call(
        functools.partial(pre_kernel, len(flat)),
        "head_pre_first",
        (len(pieces),),
        index,
        [whole((half, depth))] * len(flat) + [weight] * 2,
        [whole((2 * half, units))] * 2,
        [shape] * 2,
        flat + [gate_t, up_t],
        8 * half * depth * units * len(pieces),
        56,
    )


def act_kernel(index, own, mate, gate_w, up_w, pre, lin, ghid_own, ghid_mate, dgate, dup):
    half = own.shape[0]
    value = jnp.concatenate([own[...], mate[...]], 0)
    gate = pre[...] + dot_nt(value, gate_w[...])
    up = lin[...] + dot_nt(value, up_w[...])
    for side, ghid in enumerate((ghid_own, ghid_mate)):
        rows = slice(side * half, side * half + half)
        g, u, h = gate[rows], up[rows], ghid[0]
        sig = jax.nn.sigmoid(g)
        dgate[rows] = (h * u * (sig * (1.0 + g * (1.0 - sig)))).astype(BF)
        dup[rows] = (h * (g * sig)).astype(BF)


def act_product(index, offset, own, mate, gate_t, up_t, pre, lin, ghid, core_at):
    half, depth = own.shape
    units = gate_t.shape[0]
    weight = pl.BlockSpec((units, depth), lambda i, index: (0, index[offset]))
    ghid = ghid.reshape(2, half, units)
    ghid_own = pl.BlockSpec((1, half, units), lambda i, index: (index[core_at], 0, 0))
    ghid_mate = pl.BlockSpec((1, half, units), lambda i, index: (index[core_at + 1], 0, 0))
    return call(
        act_kernel,
        "head_act",
        (1,),
        index,
        [whole((half, depth))] * 2 + [weight] * 2 + [whole((2 * half, units))] * 2 + [ghid_own, ghid_mate],
        [whole((2 * half, units))] * 2,
        [jax.ShapeDtypeStruct((2 * half, units), BF)] * 2,
        [own, mate, gate_t, up_t, pre, lin, ghid, ghid],
        8 * half * depth * units,
        56,
    )


def back_kernel(places, place_at, index, dgate, dup, gate_w, up_w, cot, own, mate):
    product = dot_nn(dgate[...], gate_w[...]) + dot_nn(dup[...], up_w[...])
    half, depth = product.shape[0] // 2, product.shape[1]
    mate[0] = product[half:].astype(BF)
    extra = jnp.concatenate([cot[j, 0] for j in range(cot.shape[0])], 1).astype(F32)
    rows = product[:half].reshape(places, half // places, depth)
    at = lax.broadcasted_iota(jnp.int32, rows.shape, 0)
    rows = rows + jnp.where(at == index[place_at], extra[None], 0.0)
    own[0] = rows.reshape(half, depth).astype(BF)


def back_product(index, offset, count, dgate, dup, gate_t, up_t, cot, places, core_at):
    rows, units = dgate.shape
    parts, _, cot_width = cot.shape
    per = gate_t.shape[1] // cot_width
    groups = core_at
    depth = gate_t.shape[1] // groups
    per = depth // cot_width
    half = rows // 2
    cot = cot.reshape(parts, 2 * places, half // places, cot_width)
    weight = pl.BlockSpec((units, depth), lambda i, index: (0, index[offset + i]))
    cot_spec = pl.BlockSpec(
        (per, 1, half // places, cot_width), lambda i, index: (index[offset + i], index[core_at + 2], 0, 0)
    )
    out = pl.BlockSpec((1, half, depth), lambda i, index: (i, 0, 0))
    return call(
        functools.partial(back_kernel, places, core_at + 3),
        "head_back",
        (count,),
        index,
        [whole((rows, units))] * 2 + [weight] * 2 + [cot_spec],
        [out] * 2,
        [jax.ShapeDtypeStruct((count, half, depth), BF)] * 2,
        [dgate, dup, gate_t, up_t, cot],
        4 * rows * units * depth * count,
        48,
    )


def make_body(plan):
    groups, places = plan.groups, plan.places

    def body(tokens, trunk_gate, trunk_up, trunk_down, head_gate, head_up, head_down, head_grads):
        g = lax.axis_index("group")
        m = lax.axis_index("mp")
        z, c = m // 2, m % 2
        total_rows, width = tokens.shape
        rows = total_rows // plan.members
        units = trunk_gate.shape[1]
        half_rows = places * rows
        share = total_rows // groups
        offsets = [g ^ k for k in range(groups)]
        index = jnp.stack(offsets + [c, 1 - c, c * places + z, z]).astype(jnp.int32)

        toks = tokens.reshape(places, 2, rows, width).transpose(1, 0, 2, 3)
        own_tok = row(row(toks, c), z)
        toks = toks.reshape(total_rows, width)
        cot_width = head_grads.shape[2]
        cot_own = head_grads[0].reshape(places, 2, rows, cot_width).transpose(1, 0, 2, 3)
        cot_own, toks = lax.optimization_barrier((cot_own.reshape(total_rows, cot_width), toks))
        cot = lax.all_gather(cot_own, "mp", axis=0, tiled=False)

        def in_order(pieces):
            out = jnp.zeros((groups, 2, share // 2, units), BF)
            for k, pair in pieces.items():
                if isinstance(pair, tuple):
                    for side in range(2):
                        out = lax.dynamic_update_slice(out, pair[side][None, None], (g ^ k, side, 0, 0))
                else:
                    out = lax.dynamic_update_slice(out, pair[None], (g ^ k, 0, 0, 0))
            return out.reshape(total_rows, units)

        def order(first):
            return [k for k in range(groups) if not k & first] + [k for k in range(groups) if k & first]

        gate_keep, gate_send = chunks_product(index, toks, trunk_gate.T, order(1), "trunk_gate")
        up_keep, up_send = chunks_product(index, toks, trunk_up.T, order(2), "trunk_up")
        gate_r = plan.halving(gate_keep, gate_send, 1)
        up_r = plan.halving(up_keep, up_send, 2)
        hid_r = (jax.nn.silu(gate_r) * up_r).astype(BF)
        hidden = in_order(plan.gather(hid_r.reshape(2, share // 2, units)))
        down = dot_nn(hidden, trunk_down).astype(BF).reshape(2, half_rows, width)
        came = plan.core_swap(row(down, 1 - c))
        part = (row(down, c).astype(F32) + came.astype(F32)).astype(BF)
        summed = plan.place_sum(part.reshape(places, rows, width), z)
        shard = (own_tok.astype(F32) + summed).astype(BF)
        block = plan.place_gather(shard, z).reshape(2, half_rows // 2, width)

        wide = plan.gather(block)
        pieces = {}
        for k, pair in wide.items():
            if isinstance(pair, tuple):
                pair = jnp.stack(pair)
            own = pair.reshape(half_rows, width)
            pieces[k] = (own, plan.core_swap(own))

        gate_t, up_t = head_gate[0].T, head_up[0].T
        ghid = ghid_product(index, cot, head_down[0])
        last = groups - 1
        pre, lin = pre_product(index, {k: pieces[k] for k in range(last)}, gate_t, up_t)
        dgate, dup = act_product(index, last, *pieces[last], gate_t, up_t, pre, lin, ghid, groups)

        parts = {}
        for offset, count in ((last, 1), (1, last - 1), (0, 1)):
            own, mate = back_product(index, offset, count, dgate, dup, gate_t, up_t, cot, places, groups)
            came = plan.core_swap(mate)
            for i in range(count):
                total = own[i].astype(F32) + came[i].astype(F32)
                parts[offset + i] = total.reshape(2, half_rows // 2, width)
        cols = plan.scatter(parts)
        dshard = plan.place_sum(cols.astype(BF).reshape(places, rows, width), z).astype(BF)
        dhalf = plan.place_gather(dshard, z).reshape(half_rows, width)
        dmate = plan.core_swap(dhalf)
        grad_mid = jnp.zeros((2, half_rows, width), BF)
        grad_mid = lax.dynamic_update_index_in_dim(grad_mid, dhalf, c, 0)
        grad_mid = lax.dynamic_update_index_in_dim(grad_mid, dmate, 1 - c, 0).reshape(total_rows, width)

        low, high = chunks_product(index, grad_mid, trunk_down, list(range(groups)), "trunk_hidden_grad")
        back = jnp.concatenate([low, high], 0).reshape(groups, 2, share // 2, units)
        ghid_t = plan.scatter({k: back[k] for k in range(groups)}).reshape(share, units)
        dgate_r = (ghid_t * up_r * silu_grad(gate_r)).astype(BF)
        dup_r = (ghid_t * jax.nn.silu(gate_r)).astype(BF)
        both = plan.gather(jnp.stack([dgate_r, dup_r]))
        dgate_t = jnp.zeros((groups, share, units), BF)
        dup_t = jnp.zeros((groups, share, units), BF)
        for k, pair in both.items():
            dgate_t = lax.dynamic_update_index_in_dim(dgate_t, pair[0], g ^ k, 0)
            dup_t = lax.dynamic_update_index_in_dim(dup_t, pair[1], g ^ k, 0)
        dgate_t = dgate_t.reshape(total_rows, units)
        dup_t = dup_t.reshape(total_rows, units)
        back_in = (dot_nt(dgate_t, trunk_gate) + dot_nt(dup_t, trunk_up)).astype(BF)
        back_in = back_in.reshape(2, half_rows, width)
        came = plan.core_swap(row(back_in, 1 - c))
        part = (row(back_in, c).astype(F32) + came.astype(F32)).astype(BF)
        summed = plan.place_sum(part.reshape(places, rows, width), z)
        grad_x = (dshard.astype(F32) + summed).astype(BF)
        grad_gate = dot(toks, dgate_t, ((0,), (0,)))
        grad_up = dot(toks, dup_t, ((0,), (0,)))
        grad_down = dot(hidden, grad_mid, ((0,), (0,)))
        return (grad_x, grad_gate, grad_up, grad_down)

    return body


def solution(mesh):
    return jax.shard_map(
        make_body(Plan(mesh)),
        mesh=mesh,
        in_specs=(
            P(None, "group"),
            P("group", "mp"),
            P("group", "mp"),
            P("mp", "group"),
            P("group", None, "mp"),
            P("group", None, "mp"),
            P("group", "mp", None),
            P("group", None, "mp"),
        ),
        out_specs=(P("mp", "group"), P("group", "mp"), P("group", "mp"), P("mp", "group")),
        check_vma=False,
    )
```

```python
import functools

import jax
import jax.numpy as jnp
from jax import lax
from jax.experimental import pallas as pl
from jax.experimental.pallas import tpu as pltpu
from jax.sharding import PartitionSpec as P

BF = jnp.bfloat16
F32 = jnp.float32
MIB = 1 << 20


def silu_grad(pre_act):
    sig = jax.nn.sigmoid(pre_act)
    return sig * (1.0 + pre_act * (1.0 - sig))


def dot(left, right, dims):
    return lax.dot_general(left, right, (dims, ((), ())), preferred_element_type=F32)


def dot_nt(left, right):
    return dot(left, right, ((1,), (1,)))


def dot_nn(left, right):
    return dot(left, right, ((1,), (0,)))


def row(stack, index):
    return lax.dynamic_index_in_dim(stack, index, 0, keepdims=False)


def whole(shape):
    return pl.BlockSpec(shape, lambda *_: (0,) * len(shape), pipeline_mode=pl.Buffered(1))


def tie(*values):
    return lax.optimization_barrier(values)


def call(kernel, name, grid, index, in_specs, out_specs, out_shape, operands, flops, vmem, scratch=()):
    moved = sum(o.size * o.dtype.itemsize for o in operands)
    return pl.pallas_call(
        kernel,
        grid_spec=pltpu.PrefetchScalarGridSpec(
            num_scalar_prefetch=1, grid=grid, in_specs=in_specs, out_specs=out_specs, scratch_shapes=scratch
        ),
        out_shape=out_shape,
        name=name,
        cost_estimate=pl.CostEstimate(flops=flops, bytes_accessed=moved, transcendentals=0),
        compiler_params=pltpu.CompilerParams(vmem_limit_bytes=vmem * MIB),
    )(index, *operands)


class Plan:
    def __init__(self, mesh):
        self.groups = mesh.shape["group"]
        self.members = mesh.shape["mp"]
        self.places = self.members // 2

    def group_swap(self, value, mask):
        return lax.ppermute(value, "group", [(i, i ^ mask) for i in range(self.groups)])

    def core_swap(self, value):
        return lax.ppermute(value, "mp", [(i, i ^ 1) for i in range(self.members)])

    def place_swap(self, value, mask):
        return lax.ppermute(value, "mp", [(i, i ^ (2 * mask)) for i in range(self.members)])

    def hop_one(self, pair):
        reach = (1, 2) if self.groups == 4 else range(1, self.groups)
        return {0: pair} | {k: self.group_swap(pair, k) for k in reach}

    def hop_two(self, have):
        if self.groups != 4:
            return {}
        return {3: (self.group_swap(have[2][0], 1), self.group_swap(have[1][1], 2))}

    def gather(self, pair, first=None, second=None):
        have = self.hop_one(pair)
        done = first() if first else ()
        have, done = lax.optimization_barrier((have, tuple(done)))
        rest = self.hop_two(have)
        done = second(have, done) if second else done
        rest, done = lax.optimization_barrier((rest, tuple(done)))
        return have | rest, done

    def scatter(self, make, hold):
        if self.groups == 4:
            send, hold = lax.optimization_barrier((make(3, 1, None, hold)[3].astype(BF), hold))
            hops = (self.group_swap(send[0], 1), self.group_swap(send[1], 2))
            parts, hops = make(1, 2, hops, hold)
            to_x = jnp.stack([parts[1][0].astype(F32), parts[1][1].astype(F32) + hops[1].astype(F32)]).astype(BF)
            to_y = jnp.stack([parts[2][0].astype(F32) + hops[0].astype(F32), parts[2][1].astype(F32)]).astype(BF)
            to_x, to_y, hold = lax.optimization_barrier((to_x, to_y, hold))
            came_x = self.group_swap(to_x, 1)
            came_y = self.group_swap(to_y, 2)
            parts = make(0, 1, None, hold)
            return parts[0].astype(F32) + (came_x.astype(F32) + came_y.astype(F32))
        parts = make(0, self.groups, None, hold)
        total = parts[0].astype(F32)
        for k in range(1, self.groups):
            total = total + self.group_swap(parts[k].astype(BF), k).astype(F32)
        return total

    def halving(self, keep, send, first):
        current = keep.astype(F32) + self.group_swap(send, first).astype(F32)
        keys = [k for k in range(self.groups) if not k & first]
        current = {k: current[i] for i, k in enumerate(keys)}
        mask = 1
        while mask < self.groups:
            if mask != first:
                keys = [k for k in current if not k & mask]
                came = self.group_swap(jnp.stack([current[k | mask] for k in keys]).astype(BF), mask)
                current = {k: current[k] + came[i].astype(F32) for i, k in enumerate(keys)}
            mask *= 2
        return current[0]

    def place_sum(self, parts, me, beside=()):
        total = row(parts, me).astype(F32)
        came = [self.place_swap(row(parts, me ^ mask).astype(BF), mask) for mask in range(1, self.places)]
        came = tie(*came, *beside)
        for piece in came[: self.places - 1]:
            total = total + piece.astype(F32)
        return total, came[self.places - 1 :]

    def place_gather(self, piece, me, beside=()):
        came = [self.place_swap(piece, mask) for mask in range(1, self.places)]
        came, beside = lax.optimization_barrier((came, beside))
        out = jnp.zeros((self.places,) + piece.shape, piece.dtype)
        out = lax.dynamic_update_index_in_dim(out, piece, me, 0)
        for mask in range(1, self.places):
            out = lax.dynamic_update_index_in_dim(out, came[mask - 1], me ^ mask, 0)
        return out, beside


def chunks_kernel(index, *refs):
    value = jnp.concatenate([ref[...] for ref in refs[:-2]], 0)
    refs[-1][...] = dot_nt(value, refs[-2][...]).astype(BF)


def chunks_product(index, value, weight_t, order, groups, name):
    n = len(order)
    rows, depth = value.shape
    units = weight_t.shape[0]
    share = rows // groups
    specs = [pl.BlockSpec((share, depth), lambda i, index, k=k: (index[k], 0)) for k in order]
    shape = (n * share, units)
    out = call(
        chunks_kernel,
        name,
        (1,),
        index,
        specs + [whole(weight_t.shape)],
        whole(shape),
        jax.ShapeDtypeStruct(shape, BF),
        [value] * n + [weight_t],
        2 * n * share * depth * units,
        32,
    )
    return out.reshape(n, share, units)


def ghid_kernel(index, cot, weight, out):
    product = dot_nt(cot[0], weight[...])

    @pl.when(pl.program_id(0) == 0)
    def _():
        out[...] = product

    @pl.when(pl.program_id(0) > 0)
    def _():
        out[...] += product


def ghid_product(index, half_at, cot, weight):
    parts, rows, depth = cot.shape
    units = weight.shape[0]
    half = rows // 2
    return call(
        ghid_kernel,
        "head_hidden_grad",
        (parts,),
        index,
        [
            pl.BlockSpec((1, half, depth), lambda i, index: (i, index[half_at], 0)),
            pl.BlockSpec((units, depth), lambda i, index: (0, i)),
        ],
        whole((half, units)),
        jax.ShapeDtypeStruct((half, units), F32),
        [cot, weight],
        2 * half * units * depth * parts,
        40,
    )


def pre_kernel(n, begun, index, *refs):
    pieces, (gate_w, up_w), refs = refs[:n], refs[n : n + 2], refs[n + 2 :]
    start, (pre, lin) = refs[:begun], refs[begun:]
    for j in range(n // 2):

        @pl.when(pl.program_id(0) == j)
        def _(j=j):
            value = jnp.concatenate([p[...] for p in pieces[2 * j : 2 * j + 2]], 0)
            a, b = dot_nt(value, gate_w[...]), dot_nt(value, up_w[...])
            if j == 0 and begun:
                pre[...] = start[0][...] + a
                lin[...] = start[1][...] + b
            elif j == 0:
                pre[...] = a
                lin[...] = b
            else:
                pre[...] += a
                lin[...] += b


def pre_product(index, offset, pieces, gate_t, up_t, start=()):
    flat = [piece for pair in pieces for piece in pair]
    half, depth = flat[0].shape
    units = gate_t.shape[0]
    weight = pl.BlockSpec((units, depth), lambda i, index: (0, index[offset + i]))
    shape = jax.ShapeDtypeStruct((2 * half, units), F32)
    both = [whole((2 * half, units))] * 2
    return call(
        functools.partial(pre_kernel, len(flat), len(start)),
        "head_pre",
        (len(pieces),),
        index,
        [whole((half, depth))] * len(flat) + [weight] * 2 + both[: len(start)],
        both,
        [shape] * 2,
        flat + [gate_t, up_t, *start],
        8 * half * depth * units * len(pieces),
        60,
    )


def back_rows(places, place, product, cot, own, mate):
    half, depth = product.shape[0] // 2, product.shape[1]
    mate[0] = product[half:].astype(BF)
    extra = jnp.concatenate([cot[j, 0] for j in range(cot.shape[0])], 1).astype(F32)
    rows = product[:half].reshape(places, half // places, depth)
    at = lax.broadcasted_iota(jnp.int32, rows.shape, 0)
    rows = rows + jnp.where(at == place, extra[None], 0.0)
    own[0] = rows.reshape(half, depth).astype(BF)


def act_kernel(n, places, place_at, index, *refs):
    pieces, (gate_w, up_w, pre, lin, ghid_own, ghid_mate, cot, dgate, dup, own, mate) = refs[:n], refs[n : n + 11]
    sums = refs[n + 11 :]
    half = pieces[0].shape[0]
    for j in range(n // 2):

        @pl.when(pl.program_id(0) == j)
        def _(j=j):
            for side, ghid in enumerate((ghid_own, ghid_mate)):
                rows = slice(side * half, side * half + half)
                value = pieces[2 * j + side][...]
                before = (pre, lin) if j == 0 else sums
                gate = before[0][rows] + dot_nt(value, gate_w[...])
                up = before[1][rows] + dot_nt(value, up_w[...])
                if j < n // 2 - 1:
                    sums[0][rows] = gate
                    sums[1][rows] = up
                else:
                    h, sig = ghid[...], jax.nn.sigmoid(gate)
                    dgate[rows] = (h * up * (sig * (1.0 + gate * (1.0 - sig)))).astype(BF)
                    dup[rows] = (h * (gate * sig)).astype(BF)
            if j == n // 2 - 1:
                product = dot_nn(dgate[...], gate_w[...]) + dot_nn(dup[...], up_w[...])
                back_rows(places, index[place_at], product, cot, own, mate)


def cot_blocks(cot, places, groups):
    parts, rows, width = cot.shape
    return cot.reshape(parts, 2 * places, rows // (2 * places), width), (parts // groups, 1, rows // (2 * places), width)


def act_product(index, offset, pieces, gate_t, up_t, pre, lin, ghids, cot, places, core_at):
    flat = [piece for pair in pieces for piece in pair]
    half, depth = flat[0].shape
    units = gate_t.shape[0]
    last = offset + len(pieces) - 1
    weight = pl.BlockSpec((units, depth), lambda i, index: (0, index[offset + i]))
    cot, block = cot_blocks(cot, places, core_at)
    cot_spec = pl.BlockSpec(block, lambda i, index: (index[last], index[core_at + 2], 0, 0))
    return call(
        functools.partial(act_kernel, len(flat), places, core_at + 3),
        "head_act",
        (len(pieces),),
        index,
        [whole((half, depth))] * len(flat)
        + [weight] * 2
        + [whole((2 * half, units))] * 2
        + [whole((half, units))] * 2
        + [cot_spec],
        [whole((2 * half, units))] * 2 + [whole((1, half, depth))] * 2,
        [jax.ShapeDtypeStruct((2 * half, units), BF)] * 2 + [jax.ShapeDtypeStruct((1, half, depth), BF)] * 2,
        [*flat, gate_t, up_t, pre, lin, *ghids, cot],
        8 * half * depth * units * (len(pieces) + 1),
        60,
        [pltpu.VMEM((2 * half, units), F32)] * 2,
    )


def back_kernel(places, place_at, index, dgate, dup, gate_w, up_w, cot, own, mate):
    product = dot_nn(dgate[...], gate_w[...]) + dot_nn(dup[...], up_w[...])
    back_rows(places, index[place_at], product, cot, own, mate)


def back_product(index, offset, count, dgate, dup, gate_t, up_t, cot, places, core_at):
    rows, units = dgate.shape
    depth = gate_t.shape[1] // core_at
    half = rows // 2
    cot, block = cot_blocks(cot, places, core_at)
    weight = pl.BlockSpec((units, depth), lambda i, index: (0, index[offset + i]))
    cot_spec = pl.BlockSpec(block, lambda i, index: (index[offset + i], index[core_at + 2], 0, 0))
    out = pl.BlockSpec((1, half, depth), lambda i, index: (i, 0, 0))
    return call(
        functools.partial(back_kernel, places, core_at + 3),
        "head_back",
        (count,),
        index,
        [whole((rows, units))] * 2 + [weight] * 2 + [cot_spec],
        [out] * 2,
        [jax.ShapeDtypeStruct((count, half, depth), BF)] * 2,
        [dgate, dup, gate_t, up_t, cot],
        4 * rows * units * depth * count,
        48,
    )


def trunk_act_kernel(groups, core_at, index, *refs):
    ghids, gates, ups = refs[: 2 * groups], refs[2 * groups : 3 * groups], refs[3 * groups : 4 * groups]
    gate_w, up_w, dgate, dup, own, mate = refs[4 * groups :]
    for k in range(groups):
        share = gates[k].shape[0]
        ghid = jnp.concatenate([ghids[2 * k][...], ghids[2 * k + 1][...]], 0).astype(F32)
        gate, up = gates[k][...].astype(F32), ups[k][...].astype(F32)
        sig = jax.nn.sigmoid(gate)
        rows = pl.ds(pl.multiple_of(index[k] * share, share), share)
        dgate[rows] = (ghid * up * (sig * (1.0 + gate * (1.0 - sig)))).astype(BF)
        dup[rows] = (ghid * (gate * sig)).astype(BF)
    half = own.shape[0]
    for side, out in enumerate((own, mate)):
        rows = pl.ds(pl.multiple_of(index[core_at + side] * half, half), half)
        product = dot_nn(dgate[rows], gate_w[...]) + dot_nn(dup[rows], up_w[...])
        out[...] = product.astype(BF)


def trunk_act(index, ghids, gates, ups, gate_t, up_t):
    groups = len(gates)
    share, units = gates[0].shape
    rows, width = share * groups, gate_t.shape[1]
    flat = [half for pair in ghids for half in pair]
    shapes = [(rows, units)] * 2 + [(rows // 2, width)] * 2
    return call(
        functools.partial(trunk_act_kernel, groups, groups),
        "trunk_act",
        (1,),
        index,
        [whole(v.shape) for v in [*flat, *gates, *ups, gate_t, up_t]],
        [whole(shape) for shape in shapes],
        [jax.ShapeDtypeStruct(shape, BF) for shape in shapes],
        [*flat, *gates, *ups, gate_t, up_t],
        4 * rows * units * width,
        36,
    )


def grads_kernel(index, dgate, dup, toks, gate, up):
    gate[...] = dot(dgate[...], toks[...], ((0,), (0,)))
    up[...] = dot(dup[...], toks[...], ((0,), (0,)))


def grads_product(index, dgate, dup, toks):
    rows, units = dgate.shape
    width = toks.shape[1]
    tile = width // 2
    out = pl.BlockSpec((units, tile), lambda i, index: (0, i))
    return call(
        grads_kernel,
        "trunk_weight_grads",
        (2,),
        index,
        [whole((rows, units))] * 2 + [pl.BlockSpec((rows, tile), lambda i, index: (0, i))],
        [out] * 2,
        [jax.ShapeDtypeStruct((units, width), F32)] * 2,
        [dgate, dup, toks],
        4 * rows * units * width,
        48,
    )


def make_body(plan):
    groups, places = plan.groups, plan.places

    def body(tokens, trunk_gate, trunk_up, trunk_down, head_gate, head_up, head_down, head_grads):
        g = lax.axis_index("group")
        m = lax.axis_index("mp")
        z, c = m // 2, m % 2
        total_rows, width = tokens.shape
        rows = total_rows // plan.members
        units = trunk_gate.shape[1]
        half_rows = places * rows
        share = total_rows // groups
        offsets = [g ^ k for k in range(groups)]
        index = jnp.stack(offsets + [c, 1 - c, c * places + z, z]).astype(jnp.int32)

        toks = tokens.reshape(places, 2, rows, width).transpose(1, 0, 2, 3)
        own_tok = row(row(toks, c), z)
        toks = toks.reshape(total_rows, width)
        cot_width = head_grads.shape[2]
        cot_own = head_grads[0].reshape(places, 2, rows, cot_width).transpose(1, 0, 2, 3)
        cot_own, toks = lax.optimization_barrier((cot_own.reshape(total_rows, cot_width), toks))
        cot = lax.all_gather(cot_own, "mp", axis=0, tiled=False)

        def in_order(pieces):
            out = jnp.zeros((groups, 2, share // 2, units), BF)
            for k, pair in pieces.items():
                if isinstance(pair, tuple):
                    for side in range(2):
                        out = lax.dynamic_update_slice(out, pair[side][None, None], (g ^ k, side, 0, 0))
                else:
                    out = lax.dynamic_update_slice(out, pair[None], (g ^ k, 0, 0, 0))
            return out.reshape(total_rows, units)

        def sums(weight, first, name):
            keep = [k for k in range(groups) if not k & first]
            send = [k for k in range(groups) if k & first]
            sent = chunks_product(index, toks, weight.T, send, groups, name)
            return sent, lambda: chunks_product(index, toks, weight.T, keep, groups, name)

        gate_send, gate_keep = sums(trunk_gate, 1, "trunk_gate")
        up_send, up_keep = sums(trunk_up, 2, "trunk_up")
        gate_r = plan.halving(gate_keep(), gate_send, 1)
        up_r = plan.halving(up_keep(), up_send, 2)
        hid_r = (jax.nn.silu(gate_r) * up_r).astype(BF)
        hidden = in_order(plan.gather(hid_r.reshape(2, share // 2, units))[0])
        sides = hidden.reshape(2, half_rows, units)
        came = plan.core_swap(dot_nn(row(sides, 1 - c), trunk_down).astype(BF))
        part = (dot_nn(row(sides, c), trunk_down) + came.astype(F32)).astype(BF)
        part, cot, pair = tie(part, cot, jnp.stack([gate_r, up_r]).astype(BF))
        have = plan.hop_one(pair)
        ghid_own = ghid_product(index, groups, cot, head_down[0])
        beside = (ghid_own, *(have[k] for k in sorted(have)))
        summed, (ghid_own, *got) = plan.place_sum(part.reshape(places, rows, width), z, beside)
        have = dict(zip(sorted(have), got))
        shard = (own_tok.astype(F32) + summed).astype(BF)
        shard, have, cot = lax.optimization_barrier((shard, have, cot))
        rest = plan.hop_two(have)
        ghid_mate = ghid_product(index, groups + 1, cot, head_down[0])
        block, (ghid_mate, rest) = plan.place_gather(shard, z, (ghid_mate, rest))
        have = have | rest
        gates, ups = ([have[k][i] for k in range(groups)] for i in range(2))
        block = block.reshape(2, half_rows // 2, width)

        gate_t, up_t = head_gate[0].T, head_up[0].T
        def both_cores(pair):
            own = (jnp.stack(pair) if isinstance(pair, tuple) else pair).reshape(half_rows, width)
            return own, plan.core_swap(own)

        def first_product():
            return pre_product(index, 0, [both_cores(block)], gate_t, up_t)

        def second_product(have, begun):
            return pre_product(index, 1, [both_cores(have[1])], gate_t, up_t, begun)

        wide, (pre, lin) = plan.gather(block, first_product, second_product)
        pieces = [both_cores(wide[k]) for k in range(2, groups)]
        dgate, dup, *last_block = act_product(
            index, 2, pieces, gate_t, up_t, pre, lin, (ghid_own, ghid_mate), cot, places, groups
        )

        def make(offset, count, hops, hold):
            if groups == 4 and offset == groups - 1:
                own, mate = last_block
            else:
                own, mate = back_product(index, offset, count, *hold, gate_t, up_t, cot, places, groups)
            if hops is not None:
                own, mate, hops = lax.optimization_barrier((own, mate, hops))
            total = own.astype(F32) + plan.core_swap(mate).astype(F32)
            parts = {offset + i: total[i].reshape(2, half_rows // 2, width) for i in range(count)}
            return parts if hops is None else (parts, hops)

        cols = plan.scatter(make, (dgate, dup))
        dshard = plan.place_sum(cols.astype(BF).reshape(places, rows, width), z)[0].astype(BF)
        dhalf = plan.place_gather(dshard, z)[0].reshape(half_rows, width)
        dmate = plan.core_swap(dhalf)
        grad_mid = jnp.zeros((2, half_rows, width), BF)
        grad_mid = lax.dynamic_update_index_in_dim(grad_mid, dhalf, c, 0)
        grad_mid = lax.dynamic_update_index_in_dim(grad_mid, dmate, 1 - c, 0).reshape(total_rows, width)

        back = chunks_product(index, grad_mid, trunk_down, list(range(groups)), groups, "trunk_hidden_grad")
        back = back.reshape(groups, 2, share // 2, units)

        def chunks(offset, count, hops, hold):
            parts = {offset + i: back[offset + i] for i in range(count)}
            return parts if hops is None else (parts, hops)

        ghid_t = plan.scatter(chunks, ()).astype(BF)
        wide, (grad_down,) = plan.gather(ghid_t, lambda: (dot(hidden, grad_mid, ((0,), (0,))),))
        ghids = [wide[k] for k in range(groups)]
        dgate_t, dup_t, own, mate = trunk_act(index, ghids, gates, ups, trunk_gate.T, trunk_up.T)
        part = (own.astype(F32) + plan.core_swap(mate).astype(F32)).astype(BF)
        part, dgate_t, dup_t = tie(part, dgate_t, dup_t)
        grads = grads_product(index, dgate_t, dup_t, toks)
        summed, (grad_gate, grad_up) = plan.place_sum(part.reshape(places, rows, width), z, grads)
        grad_x = (dshard.astype(F32) + summed).astype(BF)
        grad_gate, grad_up = grad_gate.T, grad_up.T
        return (grad_x, grad_gate, grad_up, grad_down)

    return body


def solution(mesh):
    return jax.shard_map(
        make_body(Plan(mesh)),
        mesh=mesh,
        in_specs=(
            P(None, "group"),
            P("group", "mp"),
            P("group", "mp"),
            P("mp", "group"),
            P("group", None, "mp"),
            P("group", None, "mp"),
            P("group", "mp", None),
            P("group", None, "mp"),
        ),
        out_specs=(P("mp", "group"), P("group", "mp"), P("group", "mp"), P("mp", "group")),
        check_vma=False,
    )
```

```python
import functools

import jax
import jax.numpy as jnp
from jax import lax
from jax.experimental import pallas as pl
from jax.experimental.pallas import tpu as pltpu
from jax.sharding import PartitionSpec as P

BF = jnp.bfloat16
F32 = jnp.float32
MIB = 1 << 20


def silu_grad(pre_act):
    sig = jax.nn.sigmoid(pre_act)
    return sig * (1.0 + pre_act * (1.0 - sig))


def dot(left, right, dims):
    return lax.dot_general(left, right, (dims, ((), ())), preferred_element_type=F32)


def dot_nt(left, right):
    return dot(left, right, ((1,), (1,)))


def dot_nn(left, right):
    return dot(left, right, ((1,), (0,)))


def row(stack, index):
    return lax.dynamic_index_in_dim(stack, index, 0, keepdims=False)


def whole(shape):
    return pl.BlockSpec(shape, lambda *_: (0,) * len(shape), pipeline_mode=pl.Buffered(1))


def tie(*values):
    return lax.optimization_barrier(values)


def call(kernel, name, grid, index, in_specs, out_specs, out_shape, operands, flops, vmem, scratch=()):
    moved = sum(o.size * o.dtype.itemsize for o in operands)
    return pl.pallas_call(
        kernel,
        grid_spec=pltpu.PrefetchScalarGridSpec(
            num_scalar_prefetch=1, grid=grid, in_specs=in_specs, out_specs=out_specs, scratch_shapes=scratch
        ),
        out_shape=out_shape,
        name=name,
        cost_estimate=pl.CostEstimate(flops=flops, bytes_accessed=moved, transcendentals=0),
        compiler_params=pltpu.CompilerParams(vmem_limit_bytes=vmem * MIB),
    )(index, *operands)


class Plan:
    def __init__(self, mesh):
        self.groups = mesh.shape["group"]
        self.members = mesh.shape["mp"]
        self.places = self.members // 2

    def group_swap(self, value, mask):
        return lax.ppermute(value, "group", [(i, i ^ mask) for i in range(self.groups)])

    def core_swap(self, value):
        return lax.ppermute(value, "mp", [(i, i ^ 1) for i in range(self.members)])

    def place_swap(self, value, mask):
        return lax.ppermute(value, "mp", [(i, i ^ (2 * mask)) for i in range(self.members)])

    def hop_one(self, pair):
        reach = (1, 2) if self.groups == 4 else range(1, self.groups)
        return {0: pair} | {k: self.group_swap(pair, k) for k in reach}

    def hop_two(self, have):
        if self.groups != 4:
            return {}
        return {3: (self.group_swap(have[2][0], 1), self.group_swap(have[1][1], 2))}

    def gather(self, pair, first=None, second=None):
        have = self.hop_one(pair)
        done = first() if first else ()
        have, done = lax.optimization_barrier((have, tuple(done)))
        rest = self.hop_two(have)
        done = second(have, done) if second else done
        rest, done = lax.optimization_barrier((rest, tuple(done)))
        return have | rest, done

    def scatter(self, make, hold):
        if self.groups == 4:
            send, hold = lax.optimization_barrier((make(3, 1, None, hold)[3].astype(BF), hold))
            hops = (self.group_swap(send[0], 1), self.group_swap(send[1], 2))
            parts, hops = make(1, 2, hops, hold)
            to_x = jnp.stack([parts[1][0].astype(F32), parts[1][1].astype(F32) + hops[1].astype(F32)]).astype(BF)
            to_y = jnp.stack([parts[2][0].astype(F32) + hops[0].astype(F32), parts[2][1].astype(F32)]).astype(BF)
            to_x, to_y, hold = lax.optimization_barrier((to_x, to_y, hold))
            came_x = self.group_swap(to_x, 1)
            came_y = self.group_swap(to_y, 2)
            parts, (came_x, came_y) = make(0, 1, (came_x, came_y), hold)
            return parts[0].astype(F32) + (came_x.astype(F32) + came_y.astype(F32))
        parts = make(0, self.groups, None, hold)
        total = parts[0].astype(F32)
        for k in range(1, self.groups):
            total = total + self.group_swap(parts[k].astype(BF), k).astype(F32)
        return total

    def halving(self, keep, came, first):
        current = keep.astype(F32) + came.astype(F32)
        keys = [k for k in range(self.groups) if not k & first]
        current = {k: current[i] for i, k in enumerate(keys)}
        mask = 1
        while mask < self.groups:
            if mask != first:
                keys = [k for k in current if not k & mask]
                came = self.group_swap(jnp.stack([current[k | mask] for k in keys]).astype(BF), mask)
                current = {k: current[k] + came[i].astype(F32) for i, k in enumerate(keys)}
            mask *= 2
        return current[0]

    def place_sum(self, parts, beside=()):
        came = [self.place_swap(parts[k].astype(BF), k) for k in range(1, self.places)]
        came, beside = lax.optimization_barrier((came, beside))
        total = parts[0].astype(F32)
        for piece in came:
            total = total + piece.astype(F32)
        return total, beside

    def place_gather(self, piece, beside=()):
        came = [self.place_swap(piece, k) for k in range(1, self.places)]
        came, beside = lax.optimization_barrier((came, beside))
        return jnp.concatenate([piece, *came], 0), beside


def chunks_kernel(index, *refs):
    value = jnp.concatenate([ref[...] for ref in refs[:-2]], 0)
    refs[-1][...] = dot_nt(value, refs[-2][...]).astype(BF)


def chunks_product(index, value, weight_t, order, groups, name, rows_at=None):
    n = len(order)
    rows, depth = value.shape if rows_at is None else value[0].shape
    units = weight_t.shape[0]
    share = rows // groups
    specs = [pl.BlockSpec((share, depth), lambda i, index, k=k: (index[k], 0)) for k in order]
    if rows_at is not None:
        value, rows_each = value
        per = share // rows_each
        specs = [
            pl.BlockSpec((rows_each, depth), lambda i, index, k=k, b=b: (index[rows_at + per * index[k] + b], 0))
            for k in order
            for b in range(per)
        ]
    shape = (n * share, units)
    out = call(
        chunks_kernel,
        name,
        (1,),
        index,
        specs + [whole(weight_t.shape)],
        whole(shape),
        jax.ShapeDtypeStruct(shape, BF),
        [value] * len(specs) + [weight_t],
        2 * n * share * depth * units,
        32,
    )
    return out.reshape(n, share, units)


def ghid_kernel(n, begun, index, *refs):
    cots, weight, start, out = refs[:n], refs[n], refs[n + 1 : n + 1 + begun], refs[n + 1 + begun]
    for j in range(n):

        @pl.when(pl.program_id(0) == j)
        def _(j=j):
            product = dot_nt(cots[j][...], weight[...])
            if j == 0 and begun:
                out[...] = start[0][...] + product
            elif j == 0:
                out[...] = product
            else:
                out[...] += product


def ghid_product(index, members_at, cots, weight, start=()):
    keys = sorted(cots)
    n = len(keys)
    rows, depth = cots[keys[0]].shape
    units = weight.shape[0]

    def column(i, index):
        at = index[members_at + keys[0]]
        for j in range(1, n):
            at = jnp.where(i == j, index[members_at + keys[j]], at)
        return 0, at

    return call(
        functools.partial(ghid_kernel, n, len(start)),
        "head_hidden_grad",
        (n,),
        index,
        [whole((rows, depth))] * n + [pl.BlockSpec((units, depth), column)] + [whole((rows, units))] * len(start),
        whole((rows, units)),
        jax.ShapeDtypeStruct((rows, units), F32),
        [cots[k] for k in keys] + [weight, *start],
        2 * rows * units * depth * n,
        48,
    )


def down_kernel(n, index, value, weight, *refs):
    product = dot_nn(value[0], weight[...])
    if n:
        product = product + refs[0][...].astype(F32)
    refs[n][...] = product.astype(BF)


def down_product(index, side, value, weight, came=()):
    rows, units = value.shape
    half, width = rows // 2, weight.shape[1]
    return call(
        functools.partial(down_kernel, len(came)),
        "trunk_down",
        (1,),
        index,
        [
            pl.BlockSpec((1, half, units), lambda i, index: (side, 0, 0)),
            whole((units, width)),
            *[whole((half, width))] * len(came),
        ],
        whole((half, width)),
        jax.ShapeDtypeStruct((half, width), BF),
        [value.reshape(2, half, units), weight, *came],
        2 * half * units * width,
        24,
    )


def rows_kernel(index, value, out):
    out[...] = value[...]


def rows_in_order(index, rows_at, value, rows_each):
    rows, width = value.shape
    return call(
        rows_kernel,
        "rows_in_order",
        (rows // rows_each,),
        index,
        [pl.BlockSpec((rows_each, width), lambda i, index: (index[rows_at + i], 0))],
        pl.BlockSpec((rows_each, width), lambda i, index: (i, 0)),
        jax.ShapeDtypeStruct(value.shape, value.dtype),
        [value],
        rows * width,
        16,
    )


def cot_kernel(index, *refs):
    for j, ref in enumerate(refs[:-1]):

        @pl.when(pl.program_id(0) == j)
        def _(ref=ref):
            refs[-1][...] = ref[0]


def cot_columns(index, members_at, place_at, cots, rows):
    n = len(cots)
    width = cots[0].shape[1]
    mine = pl.BlockSpec((1, rows, width), lambda i, index: (index[place_at], 0, 0))
    return call(
        cot_kernel,
        "head_output_grad_rows",
        (n,),
        index,
        [mine] * n,
        pl.BlockSpec((rows, width), lambda i, index: (0, index[members_at + i])),
        jax.ShapeDtypeStruct((rows, n * width), BF),
        [cots[k].reshape(-1, rows, width) for k in range(n)],
        rows * n * width,
        32,
    )


def pre_kernel(n, begun, index, *refs):
    pieces, (gate_w, up_w), refs = refs[:n], refs[n : n + 2], refs[n + 2 :]
    start, (pre, lin) = refs[:begun], refs[begun:]
    value = jnp.concatenate([piece[...] for piece in pieces], 0)
    for i, (weight, out) in enumerate(((gate_w, pre), (up_w, lin))):
        product = dot_nt(value, weight[...])
        out[...] = start[i][...] + product if begun else product


def pre_product(index, offset, parts, gate_t, up_t, start=()):
    rows, depth = sum(part.shape[0] for part in parts), parts[0].shape[1]
    units = gate_t.shape[0]
    weight = pl.BlockSpec((units, depth), lambda i, index: (0, index[offset]), pipeline_mode=pl.Buffered(1))
    both = [whole((rows, units))] * 2
    return call(
        functools.partial(pre_kernel, len(parts), len(start)),
        "head_pre",
        (1,),
        index,
        [whole(part.shape) for part in parts] + [weight] * 2 + both[: len(start)],
        both,
        [jax.ShapeDtypeStruct((rows, units), F32)] * 2,
        [*parts, gate_t, up_t, *start],
        4 * rows * depth * units,
        48,
    )


def back_rows(product, cot, own, mate):
    half = product.shape[0] // 2
    mate[0] = product[half:].astype(BF)
    mine = cot.shape[0]
    first = product[:mine] + cot[...].astype(F32)
    own[0] = jnp.concatenate([first, product[mine:half]], 0).astype(BF)


def act_kernel(counts, places, blocks_at, index, *refs):
    n = sum(counts)
    parts, (gate_w, up_w, pre, lin, ghid, cot, dgate, dup, own, mate) = refs[:n], refs[n : n + 10]
    pre_held, lin_held, ghid_held, sems = refs[n + 10 :]
    half = own.shape[1]
    held = (pre_held, lin_held)
    copies = [pltpu.make_async_copy(pre, pre_held, sems.at[0]), pltpu.make_async_copy(lin, lin_held, sems.at[1])]
    rows_each = half // places
    for block in range(2 * places):
        into = ghid_held.at[pl.ds(block * rows_each, rows_each)]
        copies.append(pltpu.make_async_copy(ghid.at[index[blocks_at + block]], into, sems.at[2 + block]))
    for j, count in enumerate(counts):

        @pl.when(pl.program_id(0) == j)
        def _(j=j, count=count):
            if j == 0:
                for copy in copies:
                    copy.start()
            last = j == len(counts) - 1
            begin = sum(counts[:j])
            value = jnp.concatenate([part[...] for part in parts[begin : begin + count]], 0)
            products = [dot_nt(value, gate_w[...]), dot_nt(value, up_w[...])]
            if j == 0:
                for copy in copies:
                    copy.wait()
            if not last:
                for sums, product in zip(held, products):
                    sums[...] += product
            else:
                for side in range(2):
                    rows = slice(side * half, side * half + half)
                    gate = pre_held[rows] + products[0][rows]
                    up = lin_held[rows] + products[1][rows]
                    h, sig = ghid_held[rows], jax.nn.sigmoid(gate)
                    dgate[rows] = (h * up * (sig * (1.0 + gate * (1.0 - sig)))).astype(BF)
                    dup[rows] = (h * (gate * sig)).astype(BF)
                product = dot_nn(dgate[...], gate_w[...]) + dot_nn(dup[...], up_w[...])
                back_rows(product, cot, own, mate)


def act_product(index, offset, pieces, gate_t, up_t, pre, lin, ghid, cot, places, blocks_at):
    flat = [part for piece in pieces for part in piece]
    depth = flat[0].shape[1]
    rows, units = pre.shape
    half = rows // 2
    last = offset + len(pieces) - 1
    weight = pl.BlockSpec((units, depth), lambda i, index: (0, index[offset + i]))
    hbm = pl.BlockSpec(memory_space=pl.ANY)
    return call(
        functools.partial(act_kernel, [len(piece) for piece in pieces], places, blocks_at),
        "head_act",
        (len(pieces),),
        index,
        [whole(part.shape) for part in flat]
        + [weight] * 2
        + [hbm] * 3
        + [pl.BlockSpec((cot.shape[0], depth), lambda i, index: (0, index[last]))],
        [whole((rows, units))] * 2 + [whole((1, half, depth))] * 2,
        [jax.ShapeDtypeStruct((rows, units), BF)] * 2 + [jax.ShapeDtypeStruct((1, half, depth), BF)] * 2,
        [*flat, gate_t, up_t, pre, lin, ghid.reshape(2 * places, half // places, units), cot],
        4 * rows * depth * units * (len(pieces) + 1),
        60,
        [pltpu.VMEM((rows, units), F32)] * 3 + [pltpu.SemaphoreType.DMA((2 + 2 * places,))],
    )


def back_kernel(index, dgate, dup, gate_w, up_w, cot, own, mate):
    product = dot_nn(dgate[...], gate_w[...]) + dot_nn(dup[...], up_w[...])
    back_rows(product, cot, own, mate)


def back_product(index, offset, count, dgate, dup, gate_t, up_t, cot, groups):
    rows, units = dgate.shape
    depth = gate_t.shape[1] // groups
    half = rows // 2
    weight = pl.BlockSpec((units, depth), lambda i, index: (0, index[offset + i]))
    cot_spec = pl.BlockSpec((cot.shape[0], depth), lambda i, index: (0, index[offset + i]))
    out = pl.BlockSpec((1, half, depth), lambda i, index: (i, 0, 0))
    return call(
        back_kernel,
        "head_back",
        (count,),
        index,
        [whole((rows, units))] * 2 + [weight] * 2 + [cot_spec],
        [out] * 2,
        [jax.ShapeDtypeStruct((count, half, depth), BF)] * 2,
        [dgate, dup, gate_t, up_t, cot],
        4 * rows * units * depth * count,
        48,
    )


def trunk_act_kernel(groups, index, *refs):
    ghids, gates, ups = refs[: 2 * groups], refs[2 * groups : 3 * groups], refs[3 * groups : 4 * groups]
    gate_w, up_w, dgate, dup, own, mate = refs[4 * groups :]
    for k in range(groups):
        share = gates[k].shape[0]
        ghid = jnp.concatenate([ghids[2 * k][...], ghids[2 * k + 1][...]], 0).astype(F32)
        gate, up = gates[k][...].astype(F32), ups[k][...].astype(F32)
        sig = jax.nn.sigmoid(gate)
        rows = pl.ds(pl.multiple_of(index[k] * share, share), share)
        dgate[rows] = (ghid * up * (sig * (1.0 + gate * (1.0 - sig)))).astype(BF)
        dup[rows] = (ghid * (gate * sig)).astype(BF)
    half = own.shape[0]
    for side, out in enumerate((own, mate)):
        rows = slice(side * half, side * half + half)
        product = dot_nn(dgate[rows], gate_w[...]) + dot_nn(dup[rows], up_w[...])
        out[...] = product.astype(BF)


def trunk_act(index, ghids, gates, ups, gate_t, up_t):
    groups = len(gates)
    share, units = gates[0].shape
    rows, width = share * groups, gate_t.shape[1]
    flat = [half for pair in ghids for half in pair]
    shapes = [(rows, units)] * 2 + [(rows // 2, width)] * 2
    return call(
        functools.partial(trunk_act_kernel, groups),
        "trunk_act",
        (1,),
        index,
        [whole(v.shape) for v in [*flat, *gates, *ups, gate_t, up_t]],
        [whole(shape) for shape in shapes],
        [jax.ShapeDtypeStruct(shape, BF) for shape in shapes],
        [*flat, *gates, *ups, gate_t, up_t],
        4 * rows * units * width,
        36,
    )


def grads_kernel(index, dgate, dup, toks, gate, up):
    gate[...] = dot(dgate[...], toks[...], ((0,), (0,)))
    up[...] = dot(dup[...], toks[...], ((0,), (0,)))


def grads_product(index, dgate, dup, toks):
    rows, units = dgate.shape
    width = toks.shape[1]
    tile = width // 2
    out = pl.BlockSpec((units, tile), lambda i, index: (0, i))
    return call(
        grads_kernel,
        "trunk_weight_grads",
        (2,),
        index,
        [whole((rows, units))] * 2 + [pl.BlockSpec((rows, tile), lambda i, index: (0, i))],
        [out] * 2,
        [jax.ShapeDtypeStruct((units, width), F32)] * 2,
        [dgate, dup, toks],
        4 * rows * units * width,
        48,
    )


def make_body(plan):
    groups, places = plan.groups, plan.places

    def body(tokens, trunk_gate, trunk_up, trunk_down, head_gate, head_up, head_down, head_grads):
        g = lax.axis_index("group")
        m = lax.axis_index("mp")
        z, c = m // 2, m % 2
        total_rows, width = tokens.shape
        rows = total_rows // plan.members
        units = trunk_gate.shape[1]
        half_rows = places * rows
        share = total_rows // groups
        offsets = [g ^ k for k in range(groups)]
        both = [(k, side) for side in range(2) for k in range(places)]
        blocks = [(c ^ side) * places + (z ^ k) for k, side in both]
        members = [2 * (z ^ k) + (c ^ side) for k in range(places) for side in range(2)]
        blocks_at, members_at = groups, groups + plan.members
        rows_at = members_at + plan.members
        index = jnp.stack(offsets + blocks + members + [2 * (z ^ k) + (c ^ side) for k, side in both]).astype(jnp.int32)

        own_tok = row(tokens.reshape(plan.members, rows, width), m)
        cot_width = head_grads.shape[2]
        cot_own = head_grads[0].reshape(places, 2, rows, cot_width).transpose(1, 0, 2, 3)
        cot_own = cot_own.reshape(total_rows, cot_width)

        def in_order(pieces):
            out = jnp.zeros((groups, 2, share // 2, units), BF)
            for k, pair in pieces.items():
                if isinstance(pair, tuple):
                    for side in range(2):
                        out = lax.dynamic_update_slice(out, pair[side][None, None], (g ^ k, side, 0, 0))
                else:
                    out = lax.dynamic_update_slice(out, pair[None], (g ^ k, 0, 0, 0))
            return out.reshape(total_rows, units)

        def sums(weight, first, name):
            keep = [k for k in range(groups) if not k & first]
            send = [k for k in range(groups) if k & first]
            sent = chunks_product(index, (tokens, rows), weight.T, send, groups, name, rows_at)
            return sent, lambda: chunks_product(index, (tokens, rows), weight.T, keep, groups, name, rows_at)

        gate_send, gate_keep = sums(trunk_gate, 1, "trunk_gate")
        up_send, up_keep = sums(trunk_up, 2, "trunk_up")
        gate_came, up_came = plan.group_swap(gate_send, 1), plan.group_swap(up_send, 2)
        gate_kept, up_kept = gate_keep(), up_keep()
        near = [k for k in range(1, places) if not k & (k - 1)][::-1]
        far = [k for k in range(1, places) if k & (k - 1)]
        crossed = {k: plan.place_swap(cot_own, k) for k in near}
        cots = {0: cot_own, 1: plan.core_swap(cot_own)}
        ghid = ghid_product(index, members_at, cots, head_down[0])
        toks = rows_in_order(index, rows_at, tokens, rows)
        gate_came, up_came, ghid, toks = tie(gate_came, up_came, ghid, toks)
        gate_r = plan.halving(gate_kept, gate_came, 1)
        up_r = plan.halving(up_kept, up_came, 2)
        gate_r, up_r, crossed = lax.optimization_barrier((gate_r, up_r, crossed))

        def both_members(which):
            pairs = [((2 * k, crossed[k]), (2 * k + 1, plan.core_swap(crossed[k]))) for k in which]
            return dict(sum(pairs, ()))

        came_first, came_next = both_members(near[:1]), both_members(near[1:])
        for k in far:
            crossed[k] = plan.place_swap(crossed[k & (k - 1)], k & -k)
        hid_r = (jax.nn.silu(gate_r) * up_r).astype(BF)
        wide, (ghid, came_next, got) = plan.gather(
            hid_r.reshape(2, share // 2, units),
            second=lambda have, done: (
                ghid_product(index, members_at, came_first, head_down[0], (ghid,)),
                came_next,
                [crossed[k] for k in far],
            ),
        )
        crossed |= dict(zip(far, got))
        hidden = in_order(wide)
        pair = jnp.stack([gate_r, up_r]).astype(BF)
        hidden, pair = tie(hidden, pair)
        have = plan.hop_one(pair)
        came = plan.core_swap(down_product(index, 1, hidden, trunk_down))
        part = down_product(index, 0, hidden, trunk_down, (came,))
        came_last = came_next | both_members(far)
        part, came_last = lax.optimization_barrier((part, came_last))
        ghid = ghid_product(index, members_at, came_last, head_down[0], (ghid,))
        beside = (ghid, have)
        summed, (ghid, have) = plan.place_sum(part.reshape(places, rows, width), beside)
        cots |= came_first | came_last
        shard = (own_tok.astype(F32) + summed).astype(BF)
        shard, have, cots = lax.optimization_barrier((shard, have, cots))
        gate_t, up_t = head_gate[0].T, head_up[0].T
        cot_rows = cot_columns(index, members_at, blocks_at, cots, rows)
        came = {k: plan.place_swap(shard, k) for k in range(1, places)}
        inner = places // 2
        near, have = lax.optimization_barrier(({k: came[k] for k in range(1, inner)}, have))
        top = jnp.concatenate([shard] + [near[k] for k in range(1, inner)], 0)
        wide = [plan.hop_one(top), None]
        rest = plan.hop_two(have)
        far, wide[0], cot_rows = lax.optimization_barrier(
            ({k: came[k] for k in range(inner, places)}, wide[0], cot_rows)
        )
        low = jnp.concatenate([far[k] for k in range(inner, places)], 0)
        wide[1] = plan.hop_one(low)
        relayed = [plan.group_swap(wide[0][2], 1)] if groups == 4 else []

        def both_cores(parts):
            return parts + [plan.core_swap(part) for part in parts]

        pre, lin = pre_product(index, 0, both_cores([top, low]), gate_t, up_t)
        wide, rest, pre, lin = lax.optimization_barrier((wide, rest, pre, lin))
        have = have | rest
        gates, ups = ([have[k][i] for k in range(groups)] for i in range(2))
        relayed += [plan.group_swap(wide[1][1], 2)] if groups == 4 else []
        pieces = [both_cores([half[k] for half in wide]) for k in range(2, groups) if k in wide[0]]
        pre, lin = pre_product(index, 1, both_cores([half[1] for half in wide]), gate_t, up_t, (pre, lin))
        relayed, pieces, pre, lin = lax.optimization_barrier((relayed, pieces, pre, lin))
        pieces += [both_cores(relayed)] if groups == 4 else []
        dgate, dup, *last_block = act_product(
            index, 2, pieces, gate_t, up_t, pre, lin, ghid, cot_rows, places, blocks_at
        )

        def make(offset, count, hops, hold):
            if groups == 4 and offset == groups - 1:
                own, mate = last_block
            else:
                own, mate = back_product(index, offset, count, *hold, gate_t, up_t, cot_rows, groups)
            if hops is not None:
                own, mate, hops = lax.optimization_barrier((own, mate, hops))
            total = own.astype(F32) + plan.core_swap(mate).astype(F32)
            parts = {offset + i: total[i].reshape(2, half_rows // 2, width) for i in range(count)}
            return parts if hops is None else (parts, hops)

        cols = plan.scatter(make, (dgate, dup))
        dshard = plan.place_sum(cols.astype(BF).reshape(places, rows, width))[0].astype(BF)
        dhalf = plan.place_gather(dshard)[0]
        grad_mid = jnp.concatenate([dhalf, plan.core_swap(dhalf)], 0)

        back = chunks_product(index, grad_mid, trunk_down, list(range(groups)), groups, "trunk_hidden_grad")
        back = back.reshape(groups, 2, share // 2, units)

        def chunks(offset, count, hops, hold):
            parts = {offset + i: back[offset + i] for i in range(count)}
            return parts if hops is None else (parts, hops)

        ghid_t = plan.scatter(chunks, ()).astype(BF)
        wide, (grad_down,) = plan.gather(ghid_t, lambda: (dot(hidden, grad_mid, ((0,), (0,))),))
        ghids = [wide[k] for k in range(groups)]
        dgate_t, dup_t, own, mate = trunk_act(index, ghids, gates, ups, trunk_gate.T, trunk_up.T)
        part = (own.astype(F32) + plan.core_swap(mate).astype(F32)).astype(BF)
        part, dgate_t, dup_t = tie(part, dgate_t, dup_t)
        grads = grads_product(index, dgate_t, dup_t, toks)
        summed, (grad_gate, grad_up) = plan.place_sum(part.reshape(places, rows, width), grads)
        grad_x = (dshard.astype(F32) + summed).astype(BF)
        grad_gate, grad_up = grad_gate.T, grad_up.T
        return (grad_x, grad_gate, grad_up, grad_down)

    return body


def solution(mesh):
    return jax.shard_map(
        make_body(Plan(mesh)),
        mesh=mesh,
        in_specs=(
            P(None, "group"),
            P("group", "mp"),
            P("group", "mp"),
            P("mp", "group"),
            P("group", None, "mp"),
            P("group", None, "mp"),
            P("group", "mp", None),
            P("group", None, "mp"),
        ),
        out_specs=(P("mp", "group"), P("group", "mp"), P("group", "mp"), P("mp", "group")),
        check_vma=False,
    )
```

```python
import functools

import jax
import jax.numpy as jnp
from jax import lax
from jax.experimental import pallas as pl
from jax.experimental.pallas import tpu as pltpu
from jax.sharding import PartitionSpec as P

BF = jnp.bfloat16
F32 = jnp.float32
MIB = 1 << 20


def silu_grad(pre_act):
    sig = jax.nn.sigmoid(pre_act)
    return sig * (1.0 + pre_act * (1.0 - sig))


def dot(left, right, dims):
    return lax.dot_general(left, right, (dims, ((), ())), preferred_element_type=F32)


def dot_nt(left, right):
    return dot(left, right, ((1,), (1,)))


def dot_nn(left, right):
    return dot(left, right, ((1,), (0,)))


def row(stack, index):
    return lax.dynamic_index_in_dim(stack, index, 0, keepdims=False)


def whole(shape):
    return pl.BlockSpec(shape, lambda *_: (0,) * len(shape), pipeline_mode=pl.Buffered(1))


def tie(*values):
    return lax.optimization_barrier(values)


def call(kernel, name, grid, index, in_specs, out_specs, out_shape, operands, flops, vmem, scratch=()):
    moved = sum(o.size * o.dtype.itemsize for o in operands)
    return pl.pallas_call(
        kernel,
        grid_spec=pltpu.PrefetchScalarGridSpec(
            num_scalar_prefetch=1, grid=grid, in_specs=in_specs, out_specs=out_specs, scratch_shapes=scratch
        ),
        out_shape=out_shape,
        name=name,
        cost_estimate=pl.CostEstimate(flops=flops, bytes_accessed=moved, transcendentals=0),
        compiler_params=pltpu.CompilerParams(vmem_limit_bytes=vmem * MIB),
    )(index, *operands)


class Plan:
    def __init__(self, mesh):
        self.groups = mesh.shape["group"]
        self.members = mesh.shape["mp"]
        self.places = self.members // 2

    def group_swap(self, value, mask):
        return lax.ppermute(value, "group", [(i, i ^ mask) for i in range(self.groups)])

    def core_swap(self, value):
        return lax.ppermute(value, "mp", [(i, i ^ 1) for i in range(self.members)])

    def place_swap(self, value, mask):
        return lax.ppermute(value, "mp", [(i, i ^ (2 * mask)) for i in range(self.members)])

    def hop_one(self, pair):
        reach = (1, 2) if self.groups == 4 else range(1, self.groups)
        return {0: pair} | {k: self.group_swap(pair, k) for k in reach}

    def hop_two(self, have):
        if self.groups != 4:
            return {}
        return {3: (self.group_swap(have[2][0], 1), self.group_swap(have[1][1], 2))}

    def gather(self, pair, first=None, second=None):
        have = self.hop_one(pair)
        done = first() if first else ()
        have, done = lax.optimization_barrier((have, tuple(done)))
        rest = self.hop_two(have)
        done = second(have, done) if second else done
        rest, done = lax.optimization_barrier((rest, tuple(done)))
        return have | rest, done

    def scatter(self, make, hold):
        if self.groups == 4:
            send, hold = lax.optimization_barrier((make(3, 1, None, hold)[3].astype(BF), hold))
            hops = (self.group_swap(send[0], 1), self.group_swap(send[1], 2))
            parts, hops = make(1, 2, hops, hold)
            to_x = jnp.stack([parts[1][0].astype(F32), parts[1][1].astype(F32) + hops[1].astype(F32)]).astype(BF)
            to_y = jnp.stack([parts[2][0].astype(F32) + hops[0].astype(F32), parts[2][1].astype(F32)]).astype(BF)
            to_x, to_y, hold = lax.optimization_barrier((to_x, to_y, hold))
            came_x = self.group_swap(to_x, 1)
            came_y = self.group_swap(to_y, 2)
            parts, (came_x, came_y) = make(0, 1, (came_x, came_y), hold)
            return parts[0].astype(F32) + (came_x.astype(F32) + came_y.astype(F32))
        parts = make(0, self.groups, None, hold)
        total = parts[0].astype(F32)
        for k in range(1, self.groups):
            total = total + self.group_swap(parts[k].astype(BF), k).astype(F32)
        return total

    def halving(self, keep, came, first):
        current = keep.astype(F32) + came.astype(F32)
        keys = [k for k in range(self.groups) if not k & first]
        current = {k: current[i] for i, k in enumerate(keys)}
        mask = 1
        while mask < self.groups:
            if mask != first:
                keys = [k for k in current if not k & mask]
                came = self.group_swap(jnp.stack([current[k | mask] for k in keys]).astype(BF), mask)
                current = {k: current[k] + came[i].astype(F32) for i, k in enumerate(keys)}
            mask *= 2
        return current[0]

    def place_sum(self, parts, beside=()):
        came = [self.place_swap(parts[k].astype(BF), k) for k in range(1, self.places)]
        came, beside = lax.optimization_barrier((came, beside))
        total = parts[0].astype(F32)
        for piece in came:
            total = total + piece.astype(F32)
        return total, beside

    def place_gather(self, piece, beside=()):
        came = [self.place_swap(piece, k) for k in range(1, self.places)]
        came, beside = lax.optimization_barrier((came, beside))
        return jnp.concatenate([piece, *came], 0), beside


def chunks_kernel(index, *refs):
    value = jnp.concatenate([ref[...] for ref in refs[:-2]], 0)
    refs[-1][...] = dot_nt(value, refs[-2][...]).astype(BF)


def chunks_product(index, value, weight_t, order, groups, name, rows_at=None):
    n = len(order)
    rows, depth = value.shape if rows_at is None else value[0].shape
    units = weight_t.shape[0]
    share = rows // groups
    specs = [pl.BlockSpec((share, depth), lambda i, index, k=k: (index[k], 0)) for k in order]
    if rows_at is not None:
        value, rows_each = value
        per = share // rows_each
        specs = [
            pl.BlockSpec((rows_each, depth), lambda i, index, k=k, b=b: (index[rows_at + per * index[k] + b], 0))
            for k in order
            for b in range(per)
        ]
    shape = (n * share, units)
    out = call(
        chunks_kernel,
        name,
        (1,),
        index,
        specs + [whole(weight_t.shape)],
        whole(shape),
        jax.ShapeDtypeStruct(shape, BF),
        [value] * len(specs) + [weight_t],
        2 * n * share * depth * units,
        32,
    )
    return out.reshape(n, share, units)


def ghid_kernel(n, begun, index, *refs):
    cots, weight, start, out = refs[:n], refs[n], refs[n + 1 : n + 1 + begun], refs[n + 1 + begun]
    for j in range(n):

        @pl.when(pl.program_id(0) == j)
        def _(j=j):
            product = dot_nt(cots[j][...], weight[...])
            if j == 0 and begun:
                out[...] = start[0][...] + product
            elif j == 0:
                out[...] = product
            else:
                out[...] += product


def ghid_product(index, members_at, cots, weight, start=()):
    keys = sorted(cots)
    n = len(keys)
    rows, depth = cots[keys[0]].shape
    units = weight.shape[0]

    def column(i, index):
        at = index[members_at + keys[0]]
        for j in range(1, n):
            at = jnp.where(i == j, index[members_at + keys[j]], at)
        return 0, at

    return call(
        functools.partial(ghid_kernel, n, len(start)),
        "head_hidden_grad",
        (n,),
        index,
        [whole((rows, depth))] * n + [pl.BlockSpec((units, depth), column)] + [whole((rows, units))] * len(start),
        whole((rows, units)),
        jax.ShapeDtypeStruct((rows, units), F32),
        [cots[k] for k in keys] + [weight, *start],
        2 * rows * units * depth * n,
        48,
    )


def down_kernel(n, index, value, weight, *refs):
    product = dot_nn(value[0], weight[...])
    if n:
        product = product + refs[0][...].astype(F32)
    refs[n][...] = product.astype(BF)


def down_product(index, side, value, weight, came=()):
    rows, units = value.shape
    half, width = rows // 2, weight.shape[1]
    return call(
        functools.partial(down_kernel, len(came)),
        "trunk_down",
        (1,),
        index,
        [
            pl.BlockSpec((1, half, units), lambda i, index: (side, 0, 0)),
            whole((units, width)),
            *[whole((half, width))] * len(came),
        ],
        whole((half, width)),
        jax.ShapeDtypeStruct((half, width), BF),
        [value.reshape(2, half, units), weight, *came],
        2 * half * units * width,
        24,
    )


def rows_kernel(index, value, out):
    out[...] = value[...]


def rows_in_order(index, rows_at, value, rows_each):
    rows, width = value.shape
    return call(
        rows_kernel,
        "rows_in_order",
        (rows // rows_each,),
        index,
        [pl.BlockSpec((rows_each, width), lambda i, index: (index[rows_at + i], 0))],
        pl.BlockSpec((rows_each, width), lambda i, index: (i, 0)),
        jax.ShapeDtypeStruct(value.shape, value.dtype),
        [value],
        rows * width,
        16,
    )


def cot_kernel(index, *refs):
    for j, ref in enumerate(refs[:-1]):

        @pl.when(pl.program_id(0) == j)
        def _(ref=ref):
            refs[-1][...] = ref[0]


def cot_columns(index, members_at, place_at, cots, rows):
    n = len(cots)
    width = cots[0].shape[1]
    mine = pl.BlockSpec((1, rows, width), lambda i, index: (index[place_at], 0, 0))
    return call(
        cot_kernel,
        "head_output_grad_rows",
        (n,),
        index,
        [mine] * n,
        pl.BlockSpec((rows, width), lambda i, index: (0, index[members_at + i])),
        jax.ShapeDtypeStruct((rows, n * width), BF),
        [cots[k].reshape(-1, rows, width) for k in range(n)],
        rows * n * width,
        32,
    )


def pre_kernel(n, begun, index, *refs):
    pieces, (gate_w, up_w), refs = refs[:n], refs[n : n + 2], refs[n + 2 :]
    start, sums, sems = refs[:begun], refs[begun : begun + 2], refs[begun + 2 :]
    copies = [pltpu.make_async_copy(start[i], sums[i], sems[0].at[i]) for i in range(begun)]
    for copy in copies:
        copy.start()
    value = jnp.concatenate([piece[...] for piece in pieces], 0)
    for i, weight in enumerate((gate_w, up_w)):
        product = dot_nt(value, weight[...])
        if begun:
            copies[i].wait()
            sums[i][...] += product
        else:
            sums[i][...] = product


def pre_product(index, offset, parts, gate_t, up_t, start=()):
    rows, depth = sum(part.shape[0] for part in parts), parts[0].shape[1]
    units = gate_t.shape[0]
    weight = pl.BlockSpec((units, depth), lambda i, index: (0, index[offset]), pipeline_mode=pl.Buffered(1))
    return call(
        functools.partial(pre_kernel, len(parts), len(start)),
        "head_pre",
        (1,),
        index,
        [whole(part.shape) for part in parts] + [weight] * 2 + [pl.BlockSpec(memory_space=pl.ANY)] * len(start),
        [whole((rows, units))] * 2,
        [jax.ShapeDtypeStruct((rows, units), F32)] * 2,
        [*parts, gate_t, up_t, *start],
        4 * rows * depth * units,
        48,
        [pltpu.SemaphoreType.DMA((2,))] if start else [],
    )


def back_rows(product, cot, own, mate):
    half = product.shape[0] // 2
    mate[0] = product[half:].astype(BF)
    mine = cot.shape[0]
    first = product[:mine] + cot[...].astype(F32)
    own[0] = jnp.concatenate([first, product[mine:half]], 0).astype(BF)


def act_kernel(counts, places, blocks_at, index, *refs):
    n = sum(counts)
    parts, (gate_w, up_w, pre, lin, ghid, cot, dgate, dup, own, mate) = refs[:n], refs[n : n + 10]
    pre_held, lin_held, ghid_held, sems = refs[n + 10 :]
    half = own.shape[1]
    held = (pre_held, lin_held)
    copies = [pltpu.make_async_copy(pre, pre_held, sems.at[0]), pltpu.make_async_copy(lin, lin_held, sems.at[1])]
    rows_each = half // places
    for block in range(2 * places):
        into = ghid_held.at[pl.ds(block * rows_each, rows_each)]
        copies.append(pltpu.make_async_copy(ghid.at[index[blocks_at + block]], into, sems.at[2 + block]))
    for j, count in enumerate(counts):

        @pl.when(pl.program_id(0) == j)
        def _(j=j, count=count):
            if j == 0:
                for copy in copies:
                    copy.start()
            last = j == len(counts) - 1
            begin = sum(counts[:j])
            value = jnp.concatenate([part[...] for part in parts[begin : begin + count]], 0)
            products = [dot_nt(value, gate_w[...]), dot_nt(value, up_w[...])]
            if j == 0:
                for copy in copies:
                    copy.wait()
            if not last:
                for sums, product in zip(held, products):
                    sums[...] += product
            else:
                for side in range(2):
                    rows = slice(side * half, side * half + half)
                    gate = pre_held[rows] + products[0][rows]
                    up = lin_held[rows] + products[1][rows]
                    h, sig = ghid_held[rows], jax.nn.sigmoid(gate)
                    dgate[rows] = (h * up * (sig * (1.0 + gate * (1.0 - sig)))).astype(BF)
                    dup[rows] = (h * (gate * sig)).astype(BF)
                product = dot_nn(dgate[...], gate_w[...]) + dot_nn(dup[...], up_w[...])
                back_rows(product, cot, own, mate)


def act_product(index, offset, pieces, gate_t, up_t, pre, lin, ghid, cot, places, blocks_at):
    flat = [part for piece in pieces for part in piece]
    depth = flat[0].shape[1]
    rows, units = pre.shape
    half = rows // 2
    last = offset + len(pieces) - 1
    weight = pl.BlockSpec((units, depth), lambda i, index: (0, index[offset + i]))
    hbm = pl.BlockSpec(memory_space=pl.ANY)
    return call(
        functools.partial(act_kernel, [len(piece) for piece in pieces], places, blocks_at),
        "head_act",
        (len(pieces),),
        index,
        [whole(part.shape) for part in flat]
        + [weight] * 2
        + [hbm] * 3
        + [pl.BlockSpec((cot.shape[0], depth), lambda i, index: (0, index[last]))],
        [whole((rows, units))] * 2 + [whole((1, half, depth))] * 2,
        [jax.ShapeDtypeStruct((rows, units), BF)] * 2 + [jax.ShapeDtypeStruct((1, half, depth), BF)] * 2,
        [*flat, gate_t, up_t, pre, lin, ghid.reshape(2 * places, half // places, units), cot],
        4 * rows * depth * units * (len(pieces) + 1),
        60,
        [pltpu.VMEM((rows, units), F32)] * 3 + [pltpu.SemaphoreType.DMA((2 + 2 * places,))],
    )


def back_kernel(index, dgate, dup, gate_w, up_w, cot, own, mate):
    product = dot_nn(dgate[...], gate_w[...]) + dot_nn(dup[...], up_w[...])
    back_rows(product, cot, own, mate)


def back_product(index, offset, count, dgate, dup, gate_t, up_t, cot, groups):
    rows, units = dgate.shape
    depth = gate_t.shape[1] // groups
    half = rows // 2
    weight = pl.BlockSpec((units, depth), lambda i, index: (0, index[offset + i]))
    cot_spec = pl.BlockSpec((cot.shape[0], depth), lambda i, index: (0, index[offset + i]))
    out = pl.BlockSpec((1, half, depth), lambda i, index: (i, 0, 0))
    return call(
        back_kernel,
        "head_back",
        (count,),
        index,
        [whole((rows, units))] * 2 + [weight] * 2 + [cot_spec],
        [out] * 2,
        [jax.ShapeDtypeStruct((count, half, depth), BF)] * 2,
        [dgate, dup, gate_t, up_t, cot],
        4 * rows * units * depth * count,
        48,
    )


def trunk_act_kernel(groups, index, *refs):
    ghids, gates, ups = refs[: 2 * groups], refs[2 * groups : 3 * groups], refs[3 * groups : 4 * groups]
    gate_w, up_w, dgate, dup, own, mate = refs[4 * groups :]
    for k in range(groups):
        share = gates[k].shape[0]
        ghid = jnp.concatenate([ghids[2 * k][...], ghids[2 * k + 1][...]], 0).astype(F32)
        gate, up = gates[k][...].astype(F32), ups[k][...].astype(F32)
        sig = jax.nn.sigmoid(gate)
        rows = pl.ds(pl.multiple_of(index[k] * share, share), share)
        dgate[rows] = (ghid * up * (sig * (1.0 + gate * (1.0 - sig)))).astype(BF)
        dup[rows] = (ghid * (gate * sig)).astype(BF)
    half = own.shape[0]
    for side, out in enumerate((own, mate)):
        rows = slice(side * half, side * half + half)
        product = dot_nn(dgate[rows], gate_w[...]) + dot_nn(dup[rows], up_w[...])
        out[...] = product.astype(BF)


def trunk_act(index, ghids, gates, ups, gate_t, up_t):
    groups = len(gates)
    share, units = gates[0].shape
    rows, width = share * groups, gate_t.shape[1]
    flat = [half for pair in ghids for half in pair]
    shapes = [(rows, units)] * 2 + [(rows // 2, width)] * 2
    return call(
        functools.partial(trunk_act_kernel, groups),
        "trunk_act",
        (1,),
        index,
        [whole(v.shape) for v in [*flat, *gates, *ups, gate_t, up_t]],
        [whole(shape) for shape in shapes],
        [jax.ShapeDtypeStruct(shape, BF) for shape in shapes],
        [*flat, *gates, *ups, gate_t, up_t],
        4 * rows * units * width,
        36,
    )


def grads_kernel(index, dgate, dup, toks, gate, up):
    gate[...] = dot(dgate[...], toks[...], ((0,), (0,)))
    up[...] = dot(dup[...], toks[...], ((0,), (0,)))


def grads_product(index, dgate, dup, toks):
    rows, units = dgate.shape
    width = toks.shape[1]
    tile = width // 2
    out = pl.BlockSpec((units, tile), lambda i, index: (0, i))
    return call(
        grads_kernel,
        "trunk_weight_grads",
        (2,),
        index,
        [whole((rows, units))] * 2 + [pl.BlockSpec((rows, tile), lambda i, index: (0, i))],
        [out] * 2,
        [jax.ShapeDtypeStruct((units, width), F32)] * 2,
        [dgate, dup, toks],
        4 * rows * units * width,
        48,
    )


def make_body(plan):
    groups, places = plan.groups, plan.places

    def body(tokens, trunk_gate, trunk_up, trunk_down, head_gate, head_up, head_down, head_grads):
        g = lax.axis_index("group")
        m = lax.axis_index("mp")
        z, c = m // 2, m % 2
        total_rows, width = tokens.shape
        rows = total_rows // plan.members
        units = trunk_gate.shape[1]
        half_rows = places * rows
        share = total_rows // groups
        offsets = [g ^ k for k in range(groups)]
        both = [(k, side) for side in range(2) for k in range(places)]
        blocks = [(c ^ side) * places + (z ^ k) for k, side in both]
        members = [2 * (z ^ k) + (c ^ side) for k in range(places) for side in range(2)]
        blocks_at, members_at = groups, groups + plan.members
        rows_at = members_at + plan.members
        index = jnp.stack(offsets + blocks + members + [2 * (z ^ k) + (c ^ side) for k, side in both]).astype(jnp.int32)

        own_tok = row(tokens.reshape(plan.members, rows, width), m)
        cot_width = head_grads.shape[2]
        cot_own = head_grads[0].reshape(places, 2, rows, cot_width).transpose(1, 0, 2, 3)
        cot_own = cot_own.reshape(total_rows, cot_width)

        def in_order(pieces):
            out = jnp.zeros((groups, 2, share // 2, units), BF)
            for k, pair in pieces.items():
                if isinstance(pair, tuple):
                    for side in range(2):
                        out = lax.dynamic_update_slice(out, pair[side][None, None], (g ^ k, side, 0, 0))
                else:
                    out = lax.dynamic_update_slice(out, pair[None], (g ^ k, 0, 0, 0))
            return out.reshape(total_rows, units)

        def sums(weight, first, name):
            keep = [k for k in range(groups) if not k & first]
            send = [k for k in range(groups) if k & first]
            sent = chunks_product(index, (tokens, rows), weight.T, send, groups, name, rows_at)
            return sent, lambda: chunks_product(index, (tokens, rows), weight.T, keep, groups, name, rows_at)

        gate_send, gate_keep = sums(trunk_gate, 1, "trunk_gate")
        up_send, up_keep = sums(trunk_up, 2, "trunk_up")
        gate_came, up_came = plan.group_swap(gate_send, 1), plan.group_swap(up_send, 2)
        gate_kept, up_kept = gate_keep(), up_keep()
        near = [k for k in range(1, places) if not k & (k - 1)][::-1]
        far = [k for k in range(1, places) if k & (k - 1)]
        crossed = {k: plan.place_swap(cot_own, k) for k in near}
        cots = {0: cot_own, 1: plan.core_swap(cot_own)}
        ghid = ghid_product(index, members_at, cots, head_down[0])
        toks = rows_in_order(index, rows_at, tokens, rows)
        gate_came, up_came, ghid, toks = tie(gate_came, up_came, ghid, toks)
        gate_r = plan.halving(gate_kept, gate_came, 1)
        up_r = plan.halving(up_kept, up_came, 2)
        gate_r, up_r, crossed = lax.optimization_barrier((gate_r, up_r, crossed))

        def both_members(which):
            pairs = [((2 * k, crossed[k]), (2 * k + 1, plan.core_swap(crossed[k]))) for k in which]
            return dict(sum(pairs, ()))

        came_first, came_next = both_members(near[:1]), both_members(near[1:])
        for k in far:
            crossed[k] = plan.place_swap(crossed[k & (k - 1)], k & -k)
        hid_r = (jax.nn.silu(gate_r) * up_r).astype(BF)
        wide, (ghid, came_next, got) = plan.gather(
            hid_r.reshape(2, share // 2, units),
            second=lambda have, done: (
                ghid_product(index, members_at, came_first, head_down[0], (ghid,)),
                came_next,
                [crossed[k] for k in far],
            ),
        )
        crossed |= dict(zip(far, got))
        hidden = in_order(wide)
        pair = jnp.stack([gate_r, up_r]).astype(BF)
        hidden, pair = tie(hidden, pair)
        have = plan.hop_one(pair)
        came = plan.core_swap(down_product(index, 1, hidden, trunk_down))
        part = down_product(index, 0, hidden, trunk_down, (came,))
        came_last = came_next | both_members(far)
        part, came_last = lax.optimization_barrier((part, came_last))
        ghid = ghid_product(index, members_at, came_last, head_down[0], (ghid,))
        beside = (ghid, have)
        summed, (ghid, have) = plan.place_sum(part.reshape(places, rows, width), beside)
        cots |= came_first | came_last
        shard = (own_tok.astype(F32) + summed).astype(BF)
        shard, have, cots = lax.optimization_barrier((shard, have, cots))
        gate_t, up_t = head_gate[0].T, head_up[0].T
        cot_rows = cot_columns(index, members_at, blocks_at, cots, rows)
        came = {k: plan.place_swap(shard, k) for k in range(1, places)}
        inner = places // 2
        near, have = lax.optimization_barrier(({k: came[k] for k in range(1, inner)}, have))
        top = jnp.concatenate([shard] + [near[k] for k in range(1, inner)], 0)
        wide = [plan.hop_one(top), None]
        rest = plan.hop_two(have)
        far, wide[0], cot_rows = lax.optimization_barrier(
            ({k: came[k] for k in range(inner, places)}, wide[0], cot_rows)
        )
        low = jnp.concatenate([far[k] for k in range(inner, places)], 0)
        wide[1] = plan.hop_one(low)
        relayed = [plan.group_swap(wide[0][2], 1)] if groups == 4 else []

        def both_cores(parts):
            return parts + [plan.core_swap(part) for part in parts]

        pre, lin = pre_product(index, 0, both_cores([top, low]), gate_t, up_t)
        wide, rest, relayed, pre, lin = lax.optimization_barrier((wide, rest, relayed, pre, lin))
        have = have | rest
        gates, ups = ([have[k][i] for k in range(groups)] for i in range(2))
        relayed += [plan.group_swap(wide[1][1], 2)] if groups == 4 else []
        pieces = [both_cores([half[k] for half in wide]) for k in range(2, groups) if k in wide[0]]
        pre, lin = pre_product(index, 1, both_cores([half[1] for half in wide]), gate_t, up_t, (pre, lin))
        relayed, pieces, pre, lin = lax.optimization_barrier((relayed, pieces, pre, lin))
        pieces += [both_cores(relayed)] if groups == 4 else []
        dgate, dup, *last_block = act_product(
            index, 2, pieces, gate_t, up_t, pre, lin, ghid, cot_rows, places, blocks_at
        )

        def make(offset, count, hops, hold):
            if groups == 4 and offset == groups - 1:
                own, mate = last_block
            else:
                own, mate = back_product(index, offset, count, *hold, gate_t, up_t, cot_rows, groups)
            if hops is not None:
                own, mate, hops = lax.optimization_barrier((own, mate, hops))
            total = own.astype(F32) + plan.core_swap(mate).astype(F32)
            parts = {offset + i: total[i].reshape(2, half_rows // 2, width) for i in range(count)}
            return parts if hops is None else (parts, hops)

        cols = plan.scatter(make, (dgate, dup))
        dshard = plan.place_sum(cols.astype(BF).reshape(places, rows, width))[0].astype(BF)
        dhalf = plan.place_gather(dshard)[0]
        grad_mid = jnp.concatenate([dhalf, plan.core_swap(dhalf)], 0)

        back = chunks_product(index, grad_mid, trunk_down, list(range(groups)), groups, "trunk_hidden_grad")
        back = back.reshape(groups, 2, share // 2, units)

        def chunks(offset, count, hops, hold):
            parts = {offset + i: back[offset + i] for i in range(count)}
            return parts if hops is None else (parts, hops)

        ghid_t = plan.scatter(chunks, ()).astype(BF)
        wide, (grad_down,) = plan.gather(ghid_t, lambda: (dot(hidden, grad_mid, ((0,), (0,))),))
        ghids = [wide[k] for k in range(groups)]
        dgate_t, dup_t, own, mate = trunk_act(index, ghids, gates, ups, trunk_gate.T, trunk_up.T)
        part = (own.astype(F32) + plan.core_swap(mate).astype(F32)).astype(BF)
        part, dgate_t, dup_t = tie(part, dgate_t, dup_t)
        grads = grads_product(index, dgate_t, dup_t, toks)
        summed, (grad_gate, grad_up) = plan.place_sum(part.reshape(places, rows, width), grads)
        grad_x = (dshard.astype(F32) + summed).astype(BF)
        grad_gate, grad_up = grad_gate.T, grad_up.T
        return (grad_x, grad_gate, grad_up, grad_down)

    return body


def solution(mesh):
    return jax.shard_map(
        make_body(Plan(mesh)),
        mesh=mesh,
        in_specs=(
            P(None, "group"),
            P("group", "mp"),
            P("group", "mp"),
            P("mp", "group"),
            P("group", None, "mp"),
            P("group", None, "mp"),
            P("group", "mp", None),
            P("group", None, "mp"),
        ),
        out_specs=(P("mp", "group"), P("group", "mp"), P("group", "mp"), P("mp", "group")),
        check_vma=False,
    )
```

```python
import functools

import jax
import jax.numpy as jnp
from jax import lax
from jax.experimental import pallas as pl
from jax.experimental.pallas import tpu as pltpu
from jax.sharding import PartitionSpec as P

BF = jnp.bfloat16
F32 = jnp.float32
MIB = 1 << 20


def silu_grad(pre_act):
    sig = jax.nn.sigmoid(pre_act)
    return sig * (1.0 + pre_act * (1.0 - sig))


def dot(left, right, dims):
    return lax.dot_general(left, right, (dims, ((), ())), preferred_element_type=F32)


def dot_nt(left, right):
    return dot(left, right, ((1,), (1,)))


def dot_nn(left, right):
    return dot(left, right, ((1,), (0,)))


def row(stack, index):
    return lax.dynamic_index_in_dim(stack, index, 0, keepdims=False)


def whole(shape):
    return pl.BlockSpec(shape, lambda *_: (0,) * len(shape), pipeline_mode=pl.Buffered(1))


def tie(*values):
    return lax.optimization_barrier(values)


def call(kernel, name, grid, index, in_specs, out_specs, out_shape, operands, flops, vmem, scratch=()):
    moved = sum(o.size * o.dtype.itemsize for o in operands)
    return pl.pallas_call(
        kernel,
        grid_spec=pltpu.PrefetchScalarGridSpec(
            num_scalar_prefetch=1, grid=grid, in_specs=in_specs, out_specs=out_specs, scratch_shapes=scratch
        ),
        out_shape=out_shape,
        name=name,
        cost_estimate=pl.CostEstimate(flops=flops, bytes_accessed=moved, transcendentals=0),
        compiler_params=pltpu.CompilerParams(vmem_limit_bytes=vmem * MIB),
    )(index, *operands)


class Plan:
    def __init__(self, mesh):
        self.groups = mesh.shape["group"]
        self.members = mesh.shape["mp"]
        self.places = self.members // 2

    def group_swap(self, value, mask):
        return lax.ppermute(value, "group", [(i, i ^ mask) for i in range(self.groups)])

    def core_swap(self, value):
        return lax.ppermute(value, "mp", [(i, i ^ 1) for i in range(self.members)])

    def place_swap(self, value, mask):
        return lax.ppermute(value, "mp", [(i, i ^ (2 * mask)) for i in range(self.members)])

    def hop_one(self, pair):
        reach = (1, 2) if self.groups == 4 else range(1, self.groups)
        return {0: pair} | {k: self.group_swap(pair, k) for k in reach}

    def hop_two(self, have):
        if self.groups != 4:
            return {}
        return {3: (self.group_swap(have[2][0], 1), self.group_swap(have[1][1], 2))}

    def gather(self, pair, first=None, second=None):
        have = self.hop_one(pair)
        done = first() if first else ()
        have, done = lax.optimization_barrier((have, tuple(done)))
        rest = self.hop_two(have)
        done = second(have, done) if second else done
        rest, done = lax.optimization_barrier((rest, tuple(done)))
        return have | rest, done

    def scatter(self, make, hold):
        if self.groups == 4:
            send, hold = lax.optimization_barrier((make(3, 1, None, hold)[3].astype(BF), hold))
            hops = (self.group_swap(send[0], 1), self.group_swap(send[1], 2))
            parts, hops = make(1, 2, hops, hold)
            to_x = jnp.stack([parts[1][0].astype(F32), parts[1][1].astype(F32) + hops[1].astype(F32)]).astype(BF)
            to_y = jnp.stack([parts[2][0].astype(F32) + hops[0].astype(F32), parts[2][1].astype(F32)]).astype(BF)
            to_x, to_y, hold = lax.optimization_barrier((to_x, to_y, hold))
            came_x = self.group_swap(to_x, 1)
            came_y = self.group_swap(to_y, 2)
            parts, (came_x, came_y) = make(0, 1, (came_x, came_y), hold)
            return parts[0].astype(F32) + (came_x.astype(F32) + came_y.astype(F32))
        parts = make(0, self.groups, None, hold)
        total = parts[0].astype(F32)
        for k in range(1, self.groups):
            total = total + self.group_swap(parts[k].astype(BF), k).astype(F32)
        return total

    def halving(self, keep, came, first):
        current = keep.astype(F32) + came.astype(F32)
        keys = [k for k in range(self.groups) if not k & first]
        current = {k: current[i] for i, k in enumerate(keys)}
        mask = 1
        while mask < self.groups:
            if mask != first:
                keys = [k for k in current if not k & mask]
                came = self.group_swap(jnp.stack([current[k | mask] for k in keys]).astype(BF), mask)
                current = {k: current[k] + came[i].astype(F32) for i, k in enumerate(keys)}
            mask *= 2
        return current[0]

    def place_sum(self, parts, beside=()):
        came = [self.place_swap(parts[k].astype(BF), k) for k in range(1, self.places)]
        came, beside = lax.optimization_barrier((came, beside))
        total = parts[0].astype(F32)
        for piece in came:
            total = total + piece.astype(F32)
        return total, beside

    def place_gather(self, piece, beside=()):
        came = [self.place_swap(piece, k) for k in range(1, self.places)]
        came, beside = lax.optimization_barrier((came, beside))
        return jnp.concatenate([piece, *came], 0), beside


def chunks_kernel(index, *refs):
    value = jnp.concatenate([ref[...] for ref in refs[:-2]], 0)
    refs[-1][...] = dot_nt(value, refs[-2][...]).astype(BF)


def chunks_product(index, value, weight_t, order, groups, name, rows_at=None):
    n = len(order)
    rows, depth = value.shape if rows_at is None else value[0].shape
    units = weight_t.shape[0]
    share = rows // groups
    specs = [pl.BlockSpec((share, depth), lambda i, index, k=k: (index[k], 0)) for k in order]
    if rows_at is not None:
        value, rows_each = value
        per = share // rows_each
        specs = [
            pl.BlockSpec((rows_each, depth), lambda i, index, k=k, b=b: (index[rows_at + per * index[k] + b], 0))
            for k in order
            for b in range(per)
        ]
    shape = (n * share, units)
    out = call(
        chunks_kernel,
        name,
        (1,),
        index,
        specs + [whole(weight_t.shape)],
        whole(shape),
        jax.ShapeDtypeStruct(shape, BF),
        [value] * len(specs) + [weight_t],
        2 * n * share * depth * units,
        32,
    )
    return out.reshape(n, share, units)


def ghid_kernel(n, begun, index, *refs):
    cots, weight, start, out = refs[:n], refs[n], refs[n + 1 : n + 1 + begun], refs[n + 1 + begun]
    for j in range(n):

        @pl.when(pl.program_id(0) == j)
        def _(j=j):
            product = dot_nt(cots[j][...], weight[...])
            if j == 0 and begun:
                out[...] = start[0][...] + product
            elif j == 0:
                out[...] = product
            else:
                out[...] += product


def ghid_product(index, members_at, cots, weight, start=()):
    keys = sorted(cots)
    n = len(keys)
    rows, depth = cots[keys[0]].shape
    units = weight.shape[0]

    def column(i, index):
        at = index[members_at + keys[0]]
        for j in range(1, n):
            at = jnp.where(i == j, index[members_at + keys[j]], at)
        return 0, at

    return call(
        functools.partial(ghid_kernel, n, len(start)),
        "head_hidden_grad",
        (n,),
        index,
        [whole((rows, depth))] * n + [pl.BlockSpec((units, depth), column)] + [whole((rows, units))] * len(start),
        whole((rows, units)),
        jax.ShapeDtypeStruct((rows, units), F32),
        [cots[k] for k in keys] + [weight, *start],
        2 * rows * units * depth * n,
        48,
    )


def down_kernel(n, index, value, weight, *refs):
    product = dot_nn(value[0], weight[...])
    if n:
        product = product + refs[0][...].astype(F32)
    refs[n][...] = product.astype(BF)


def down_product(index, side, value, weight, came=()):
    rows, units = value.shape
    half, width = rows // 2, weight.shape[1]
    return call(
        functools.partial(down_kernel, len(came)),
        "trunk_down",
        (1,),
        index,
        [
            pl.BlockSpec((1, half, units), lambda i, index: (side, 0, 0)),
            whole((units, width)),
            *[whole((half, width))] * len(came),
        ],
        whole((half, width)),
        jax.ShapeDtypeStruct((half, width), BF),
        [value.reshape(2, half, units), weight, *came],
        2 * half * units * width,
        24,
    )


def rows_kernel(index, value, out):
    out[...] = value[...]


def rows_in_order(index, rows_at, value, rows_each):
    rows, width = value.shape
    return call(
        rows_kernel,
        "rows_in_order",
        (rows // rows_each,),
        index,
        [pl.BlockSpec((rows_each, width), lambda i, index: (index[rows_at + i], 0))],
        pl.BlockSpec((rows_each, width), lambda i, index: (i, 0)),
        jax.ShapeDtypeStruct(value.shape, value.dtype),
        [value],
        rows * width,
        16,
    )


def cot_kernel(index, *refs):
    for j, ref in enumerate(refs[:-1]):

        @pl.when(pl.program_id(0) == j)
        def _(ref=ref):
            refs[-1][...] = ref[0]


def cot_columns(index, members_at, place_at, cots, rows):
    n = len(cots)
    width = cots[0].shape[1]
    mine = pl.BlockSpec((1, rows, width), lambda i, index: (index[place_at], 0, 0))
    return call(
        cot_kernel,
        "head_output_grad_rows",
        (n,),
        index,
        [mine] * n,
        pl.BlockSpec((rows, width), lambda i, index: (0, index[members_at + i])),
        jax.ShapeDtypeStruct((rows, n * width), BF),
        [cots[k].reshape(-1, rows, width) for k in range(n)],
        rows * n * width,
        32,
    )


def pre_kernel(n, begun, index, *refs):
    pieces, (gate_w, up_w), refs = refs[:n], refs[n : n + 2], refs[n + 2 :]
    start, sums, sems = refs[:begun], refs[begun : begun + 2], refs[begun + 2 :]
    copies = [pltpu.make_async_copy(start[i], sums[i], sems[0].at[i]) for i in range(begun)]
    for copy in copies:
        copy.start()
    value = jnp.concatenate([piece[...] for piece in pieces], 0)
    for i, weight in enumerate((gate_w, up_w)):
        product = dot_nt(value, weight[...])
        if begun:
            copies[i].wait()
            sums[i][...] += product
        else:
            sums[i][...] = product


def pre_product(index, offset, parts, gate_t, up_t, start=()):
    rows, depth = sum(part.shape[0] for part in parts), parts[0].shape[1]
    units = gate_t.shape[0]
    weight = pl.BlockSpec((units, depth), lambda i, index: (0, index[offset]), pipeline_mode=pl.Buffered(1))
    return call(
        functools.partial(pre_kernel, len(parts), len(start)),
        "head_pre",
        (1,),
        index,
        [whole(part.shape) for part in parts] + [weight] * 2 + [pl.BlockSpec(memory_space=pl.ANY)] * len(start),
        [whole((rows, units))] * 2,
        [jax.ShapeDtypeStruct((rows, units), F32)] * 2,
        [*parts, gate_t, up_t, *start],
        4 * rows * depth * units,
        48,
        [pltpu.SemaphoreType.DMA((2,))] if start else [],
    )


def back_rows(product, cot, own, mate):
    half = product.shape[0] // 2
    mate[0] = product[half:].astype(BF)
    mine = cot.shape[0]
    first = product[:mine] + cot[...].astype(F32)
    own[0] = jnp.concatenate([first, product[mine:half]], 0).astype(BF)


def gradients(gate, up, hidden):
    sig = jax.nn.sigmoid(gate)
    act = gate * sig
    return (hidden * up * (sig + act * (1.0 - sig))).astype(BF), (hidden * act).astype(BF)


def act_kernel(counts, places, blocks_at, index, *refs):
    n = sum(counts)
    parts, (gate_w, up_w, pre, lin, ghid, cot, dgate, dup, own, mate) = refs[:n], refs[n : n + 10]
    gate_sum, up_sum, pre_held, lin_held, ghid_held, sems = refs[n + 10 :]
    half = own.shape[1]
    copies = [pltpu.make_async_copy(pre, pre_held, sems.at[0]), pltpu.make_async_copy(lin, lin_held, sems.at[1])]
    rows_each = half // places
    for block in range(2 * places):
        into = ghid_held.at[pl.ds(block * rows_each, rows_each)]
        copies.append(pltpu.make_async_copy(ghid.at[index[blocks_at + block]], into, sems.at[2 + block]))
    for j, count in enumerate(counts):

        @pl.when(pl.program_id(0) == j)
        def _(j=j, count=count):
            if j == 0:
                for copy in copies:
                    copy.start()
            begin = sum(counts[:j])
            value = jnp.concatenate([part[...] for part in parts[begin : begin + count]], 0)
            for sums, weight in ((gate_sum, gate_w), (up_sum, up_w)):
                if j == 0:
                    sums[...] = dot_nt(value, weight[...])
                else:
                    sums[...] += dot_nt(value, weight[...])
            if j == len(counts) - 1:
                for copy in copies:
                    copy.wait()

                @pl.loop(0, 2 * half // 16)
                def _(step):
                    rows = pl.ds(pl.multiple_of(step * 16, 16), 16)
                    gate, up = gate_sum[rows] + pre_held[rows], up_sum[rows] + lin_held[rows]
                    dgate[rows], dup[rows] = gradients(gate, up, ghid_held[rows])

                product = dot_nn(dgate[...], gate_w[...]) + dot_nn(dup[...], up_w[...])
                back_rows(product, cot, own, mate)


def act_product(index, offset, pieces, gate_t, up_t, pre, lin, ghid, cot, places, blocks_at):
    flat = [part for piece in pieces for part in piece]
    depth = flat[0].shape[1]
    rows, units = pre.shape
    half = rows // 2
    last = offset + len(pieces) - 1
    weight = pl.BlockSpec((units, depth), lambda i, index: (0, index[offset + i]))
    hbm = pl.BlockSpec(memory_space=pl.ANY)
    return call(
        functools.partial(act_kernel, [len(piece) for piece in pieces], places, blocks_at),
        "head_act",
        (len(pieces),),
        index,
        [whole(part.shape) for part in flat]
        + [weight] * 2
        + [hbm] * 3
        + [pl.BlockSpec((cot.shape[0], depth), lambda i, index: (0, index[last]))],
        [whole((rows, units))] * 2 + [whole((1, half, depth))] * 2,
        [jax.ShapeDtypeStruct((rows, units), BF)] * 2 + [jax.ShapeDtypeStruct((1, half, depth), BF)] * 2,
        [*flat, gate_t, up_t, pre, lin, ghid.reshape(2 * places, half // places, units), cot],
        4 * rows * depth * units * (len(pieces) + 1),
        60,
        [pltpu.VMEM((rows, units), F32)] * 5 + [pltpu.SemaphoreType.DMA((2 + 2 * places,))],
    )


def back_kernel(index, dgate, dup, gate_w, up_w, cot, own, mate):
    product = dot_nn(dgate[...], gate_w[...]) + dot_nn(dup[...], up_w[...])
    back_rows(product, cot, own, mate)


def back_product(index, offset, count, dgate, dup, gate_t, up_t, cot, groups):
    rows, units = dgate.shape
    depth = gate_t.shape[1] // groups
    half = rows // 2
    cut = 2
    weight = pl.BlockSpec((units, depth // cut), lambda i, j, index: (0, index[offset + i] * cut + j))
    cot_spec = pl.BlockSpec((cot.shape[0], depth // cut), lambda i, j, index: (0, index[offset + i] * cut + j))
    out = pl.BlockSpec((1, half, depth // cut), lambda i, j, index: (i, 0, j))
    return call(
        back_kernel,
        "head_back",
        (count, cut),
        index,
        [whole((rows, units))] * 2 + [weight] * 2 + [cot_spec],
        [out] * 2,
        [jax.ShapeDtypeStruct((count, half, depth), BF)] * 2,
        [dgate, dup, gate_t, up_t, cot],
        4 * rows * units * depth * count,
        48,
    )


def trunk_act_kernel(groups, index, *refs):
    ghids, gates, ups = refs[: 2 * groups], refs[2 * groups : 3 * groups], refs[3 * groups : 4 * groups]
    gate_w, up_w, dgate, dup, own, mate = refs[4 * groups :]
    for k in range(groups):
        share = gates[k].shape[0]
        for side in range(2):
            part = share // 2
            tile = 16 if part % 16 == 0 else part

            @pl.loop(0, part // tile)
            def _(step, k=k, side=side, part=part, tile=tile):
                at = pl.multiple_of(step * tile, tile)
                ghid = ghids[2 * k + side][pl.ds(at, tile)].astype(F32)
                rows = pl.ds(pl.multiple_of(side * part + at, tile), tile)
                gate, up = gates[k][rows].astype(F32), ups[k][rows].astype(F32)
                rows = pl.ds(pl.multiple_of(index[k] * share + side * part + at, tile), tile)
                dgate[rows], dup[rows] = gradients(gate, up, ghid)

    half = own.shape[0]
    for side, out in enumerate((own, mate)):
        rows = slice(side * half, side * half + half)
        product = dot_nn(dgate[rows], gate_w[...]) + dot_nn(dup[rows], up_w[...])
        out[...] = product.astype(BF)


def trunk_act(index, ghids, gates, ups, gate_t, up_t):
    groups = len(gates)
    share, units = gates[0].shape
    rows, width = share * groups, gate_t.shape[1]
    flat = [half for pair in ghids for half in pair]
    shapes = [(rows, units)] * 2 + [(rows // 2, width)] * 2
    return call(
        functools.partial(trunk_act_kernel, groups),
        "trunk_act",
        (1,),
        index,
        [whole(v.shape) for v in [*flat, *gates, *ups, gate_t, up_t]],
        [whole(shape) for shape in shapes],
        [jax.ShapeDtypeStruct(shape, BF) for shape in shapes],
        [*flat, *gates, *ups, gate_t, up_t],
        4 * rows * units * width,
        36,
    )


def grads_kernel(index, dgate, dup, toks, gate, up):
    gate[...] = dot(dgate[...], toks[...], ((0,), (0,)))
    up[...] = dot(dup[...], toks[...], ((0,), (0,)))


def grads_product(index, dgate, dup, toks):
    rows, units = dgate.shape
    width = toks.shape[1]
    tile = width // 2
    out = pl.BlockSpec((units, tile), lambda i, index: (0, i))
    return call(
        grads_kernel,
        "trunk_weight_grads",
        (2,),
        index,
        [whole((rows, units))] * 2 + [pl.BlockSpec((rows, tile), lambda i, index: (0, i))],
        [out] * 2,
        [jax.ShapeDtypeStruct((units, width), F32)] * 2,
        [dgate, dup, toks],
        4 * rows * units * width,
        48,
    )


def make_body(plan):
    groups, places = plan.groups, plan.places

    def body(tokens, trunk_gate, trunk_up, trunk_down, head_gate, head_up, head_down, head_grads):
        g = lax.axis_index("group")
        m = lax.axis_index("mp")
        z, c = m // 2, m % 2
        total_rows, width = tokens.shape
        rows = total_rows // plan.members
        units = trunk_gate.shape[1]
        half_rows = places * rows
        share = total_rows // groups
        offsets = [g ^ k for k in range(groups)]
        both = [(k, side) for side in range(2) for k in range(places)]
        blocks = [(c ^ side) * places + (z ^ k) for k, side in both]
        members = [2 * (z ^ k) + (c ^ side) for k in range(places) for side in range(2)]
        blocks_at, members_at = groups, groups + plan.members
        rows_at = members_at + plan.members
        index = jnp.stack(offsets + blocks + members + [2 * (z ^ k) + (c ^ side) for k, side in both]).astype(jnp.int32)

        own_tok = row(tokens.reshape(plan.members, rows, width), m)
        cot_width = head_grads.shape[2]
        cot_own = head_grads[0].reshape(places, 2, rows, cot_width).transpose(1, 0, 2, 3)
        cot_own = cot_own.reshape(total_rows, cot_width)

        def in_order(pieces):
            out = jnp.zeros((groups, 2, share // 2, units), BF)
            for k, pair in pieces.items():
                if isinstance(pair, tuple):
                    for side in range(2):
                        out = lax.dynamic_update_slice(out, pair[side][None, None], (g ^ k, side, 0, 0))
                else:
                    out = lax.dynamic_update_slice(out, pair[None], (g ^ k, 0, 0, 0))
            return out.reshape(total_rows, units)

        def sums(weight, first, name):
            keep = [k for k in range(groups) if not k & first]
            send = [k for k in range(groups) if k & first]
            sent = chunks_product(index, (tokens, rows), weight.T, send, groups, name, rows_at)
            return sent, lambda: chunks_product(index, (tokens, rows), weight.T, keep, groups, name, rows_at)

        gate_send, gate_keep = sums(trunk_gate, 1, "trunk_gate")
        up_send, up_keep = sums(trunk_up, 2, "trunk_up")
        gate_came, up_came = plan.group_swap(gate_send, 1), plan.group_swap(up_send, 2)
        gate_kept, up_kept = gate_keep(), up_keep()
        near = [k for k in range(1, places) if not k & (k - 1)][::-1]
        far = [k for k in range(1, places) if k & (k - 1)]
        crossed = {k: plan.place_swap(cot_own, k) for k in near}
        cots = {0: cot_own, 1: plan.core_swap(cot_own)}
        ghid = ghid_product(index, members_at, cots, head_down[0])
        toks = rows_in_order(index, rows_at, tokens, rows)
        gate_came, up_came, ghid, toks = tie(gate_came, up_came, ghid, toks)
        gate_r = plan.halving(gate_kept, gate_came, 1)
        up_r = plan.halving(up_kept, up_came, 2)
        gate_r, up_r, crossed = lax.optimization_barrier((gate_r, up_r, crossed))

        def both_members(which):
            pairs = [((2 * k, crossed[k]), (2 * k + 1, plan.core_swap(crossed[k]))) for k in which]
            return dict(sum(pairs, ()))

        came_first, came_next = both_members(near[:1]), both_members(near[1:])
        for k in far:
            crossed[k] = plan.place_swap(crossed[k & (k - 1)], k & -k)
        hid_r = (jax.nn.silu(gate_r) * up_r).astype(BF)
        wide, (ghid, came_next, got) = plan.gather(
            hid_r.reshape(2, share // 2, units),
            second=lambda have, done: (
                ghid_product(index, members_at, came_first, head_down[0], (ghid,)),
                came_next,
                [crossed[k] for k in far],
            ),
        )
        crossed |= dict(zip(far, got))
        hidden = in_order(wide)
        pair = jnp.stack([gate_r, up_r]).astype(BF)
        hidden, pair = tie(hidden, pair)
        have = plan.hop_one(pair)
        came = plan.core_swap(down_product(index, 1, hidden, trunk_down))
        part = down_product(index, 0, hidden, trunk_down, (came,))
        came_last = came_next | both_members(far)
        part, came_last = lax.optimization_barrier((part, came_last))
        ghid = ghid_product(index, members_at, came_last, head_down[0], (ghid,))
        beside = (ghid, have)
        summed, (ghid, have) = plan.place_sum(part.reshape(places, rows, width), beside)
        cots |= came_first | came_last
        shard = (own_tok.astype(F32) + summed).astype(BF)
        shard, have, cots = lax.optimization_barrier((shard, have, cots))
        gate_t, up_t = head_gate[0].T, head_up[0].T
        cot_rows = cot_columns(index, members_at, blocks_at, cots, rows)
        came = {k: plan.place_swap(shard, k) for k in range(1, places)}
        inner = places // 2
        near, have = lax.optimization_barrier(({k: came[k] for k in range(1, inner)}, have))
        top = jnp.concatenate([shard] + [near[k] for k in range(1, inner)], 0)
        wide = [plan.hop_one(top), None]
        rest = plan.hop_two(have)
        far, wide[0], cot_rows = lax.optimization_barrier(
            ({k: came[k] for k in range(inner, places)}, wide[0], cot_rows)
        )
        low = jnp.concatenate([far[k] for k in range(inner, places)], 0)
        wide[1] = plan.hop_one(low)
        relayed = [plan.group_swap(wide[0][2], 1)] if groups == 4 else []

        def both_cores(parts):
            return parts + [plan.core_swap(part) for part in parts]

        pre, lin = pre_product(index, 0, both_cores([top, low]), gate_t, up_t)
        wide, rest, relayed, pre, lin = lax.optimization_barrier((wide, rest, relayed, pre, lin))
        have = have | rest
        gates, ups = ([have[k][i] for k in range(groups)] for i in range(2))
        relayed += [plan.group_swap(wide[1][1], 2)] if groups == 4 else []
        pieces = [both_cores([half[k] for half in wide]) for k in range(2, groups) if k in wide[0]]
        pre, lin = pre_product(index, 1, both_cores([half[1] for half in wide]), gate_t, up_t, (pre, lin))
        relayed, pieces, pre, lin = lax.optimization_barrier((relayed, pieces, pre, lin))
        pieces += [both_cores(relayed)] if groups == 4 else []
        dgate, dup, *last_block = act_product(
            index, 2, pieces, gate_t, up_t, pre, lin, ghid, cot_rows, places, blocks_at
        )

        def make(offset, count, hops, hold):
            if groups == 4 and offset == groups - 1:
                own, mate = last_block
            else:
                own, mate = back_product(index, offset, count, *hold, gate_t, up_t, cot_rows, groups)
            if hops is not None:
                own, mate, hops = lax.optimization_barrier((own, mate, hops))
            total = own.astype(F32) + plan.core_swap(mate).astype(F32)
            parts = {offset + i: total[i].reshape(2, half_rows // 2, width) for i in range(count)}
            return parts if hops is None else (parts, hops)

        cols = plan.scatter(make, (dgate, dup))
        dshard = plan.place_sum(cols.astype(BF).reshape(places, rows, width))[0].astype(BF)
        dhalf = plan.place_gather(dshard)[0]
        grad_mid = jnp.concatenate([dhalf, plan.core_swap(dhalf)], 0)

        back = chunks_product(index, grad_mid, trunk_down, list(range(groups)), groups, "trunk_hidden_grad")
        back = back.reshape(groups, 2, share // 2, units)

        def chunks(offset, count, hops, hold):
            parts = {offset + i: back[offset + i] for i in range(count)}
            return parts if hops is None else (parts, hops)

        ghid_t = plan.scatter(chunks, ()).astype(BF)
        wide, (grad_down,) = plan.gather(ghid_t, lambda: (dot(hidden, grad_mid, ((0,), (0,))),))
        ghids = [wide[k] for k in range(groups)]
        dgate_t, dup_t, own, mate = trunk_act(index, ghids, gates, ups, trunk_gate.T, trunk_up.T)
        part = (own.astype(F32) + plan.core_swap(mate).astype(F32)).astype(BF)
        part, dgate_t, dup_t = tie(part, dgate_t, dup_t)
        grads = grads_product(index, dgate_t, dup_t, toks)
        summed, (grad_gate, grad_up) = plan.place_sum(part.reshape(places, rows, width), grads)
        grad_x = (dshard.astype(F32) + summed).astype(BF)
        grad_gate, grad_up = grad_gate.T, grad_up.T
        return (grad_x, grad_gate, grad_up, grad_down)

    return body


def solution(mesh):
    return jax.shard_map(
        make_body(Plan(mesh)),
        mesh=mesh,
        in_specs=(
            P(None, "group"),
            P("group", "mp"),
            P("group", "mp"),
            P("mp", "group"),
            P("group", None, "mp"),
            P("group", None, "mp"),
            P("group", "mp", None),
            P("group", None, "mp"),
        ),
        out_specs=(P("mp", "group"), P("group", "mp"), P("group", "mp"), P("mp", "group")),
        check_vma=False,
    )
```

```python
import functools

import jax
import jax.numpy as jnp
from jax import lax
from jax.experimental import pallas as pl
from jax.experimental.pallas import tpu as pltpu
from jax.sharding import PartitionSpec as P

BF = jnp.bfloat16
F32 = jnp.float32
MIB = 1 << 20


def silu_grad(pre_act):
    sig = jax.nn.sigmoid(pre_act)
    return sig * (1.0 + pre_act * (1.0 - sig))


def dot(left, right, dims):
    return lax.dot_general(left, right, (dims, ((), ())), preferred_element_type=F32)


def dot_nt(left, right):
    return dot(left, right, ((1,), (1,)))


def dot_nn(left, right):
    return dot(left, right, ((1,), (0,)))


def row(stack, index):
    return lax.dynamic_index_in_dim(stack, index, 0, keepdims=False)


def whole(shape):
    return pl.BlockSpec(shape, lambda *_: (0,) * len(shape), pipeline_mode=pl.Buffered(1))


def tie(*values):
    return lax.optimization_barrier(values)


def call(kernel, name, grid, index, in_specs, out_specs, out_shape, operands, flops, vmem, scratch=()):
    moved = sum(o.size * o.dtype.itemsize for o in operands)
    return pl.pallas_call(
        kernel,
        grid_spec=pltpu.PrefetchScalarGridSpec(
            num_scalar_prefetch=1, grid=grid, in_specs=in_specs, out_specs=out_specs, scratch_shapes=scratch
        ),
        out_shape=out_shape,
        name=name,
        cost_estimate=pl.CostEstimate(flops=flops, bytes_accessed=moved, transcendentals=0),
        compiler_params=pltpu.CompilerParams(vmem_limit_bytes=vmem * MIB),
    )(index, *operands)


class Plan:
    def __init__(self, mesh):
        self.groups = mesh.shape["group"]
        self.members = mesh.shape["mp"]
        self.places = self.members // 2

    def group_swap(self, value, mask):
        return lax.ppermute(value, "group", [(i, i ^ mask) for i in range(self.groups)])

    def core_swap(self, value):
        return lax.ppermute(value, "mp", [(i, i ^ 1) for i in range(self.members)])

    def place_swap(self, value, mask):
        return lax.ppermute(value, "mp", [(i, i ^ (2 * mask)) for i in range(self.members)])

    def hop_one(self, pair):
        reach = (1, 2) if self.groups == 4 else range(1, self.groups)
        return {0: pair} | {k: self.group_swap(pair, k) for k in reach}

    def hop_two(self, have):
        if self.groups != 4:
            return {}
        return {3: (self.group_swap(have[2][0], 1), self.group_swap(have[1][1], 2))}

    def gather(self, pair, first=None, second=None):
        have = self.hop_one(pair)
        done = first() if first else ()
        have, done = lax.optimization_barrier((have, tuple(done)))
        rest = self.hop_two(have)
        done = second(have, done) if second else done
        rest, done = lax.optimization_barrier((rest, tuple(done)))
        return have | rest, done

    def scatter(self, make, hold):
        if self.groups == 4:
            send, hold = lax.optimization_barrier((make(3, 1, None, hold)[3].astype(BF), hold))
            hops = (self.group_swap(send[0], 1), self.group_swap(send[1], 2))
            parts, hops = make(1, 2, hops, hold)
            to_x = jnp.stack([parts[1][0].astype(F32), parts[1][1].astype(F32) + hops[1].astype(F32)]).astype(BF)
            to_y = jnp.stack([parts[2][0].astype(F32) + hops[0].astype(F32), parts[2][1].astype(F32)]).astype(BF)
            to_x, to_y, hold = lax.optimization_barrier((to_x, to_y, hold))
            came_x = self.group_swap(to_x, 1)
            came_y = self.group_swap(to_y, 2)
            parts, (came_x, came_y) = make(0, 1, (came_x, came_y), hold)
            return parts[0].astype(F32) + (came_x.astype(F32) + came_y.astype(F32))
        parts = make(0, self.groups, None, hold)
        total = parts[0].astype(F32)
        for k in range(1, self.groups):
            total = total + self.group_swap(parts[k].astype(BF), k).astype(F32)
        return total

    def halving(self, keep, came, first):
        current = keep.astype(F32) + came.astype(F32)
        keys = [k for k in range(self.groups) if not k & first]
        current = {k: current[i] for i, k in enumerate(keys)}
        mask = 1
        while mask < self.groups:
            if mask != first:
                keys = [k for k in current if not k & mask]
                came = self.group_swap(jnp.stack([current[k | mask] for k in keys]).astype(BF), mask)
                current = {k: current[k] + came[i].astype(F32) for i, k in enumerate(keys)}
            mask *= 2
        return current[0]

    def place_sum(self, parts, beside=()):
        came = [self.place_swap(parts[k].astype(BF), k) for k in range(1, self.places)]
        came, beside = lax.optimization_barrier((came, beside))
        total = parts[0].astype(F32)
        for piece in came:
            total = total + piece.astype(F32)
        return total, beside

    def place_gather(self, piece, beside=()):
        came = [self.place_swap(piece, k) for k in range(1, self.places)]
        came, beside = lax.optimization_barrier((came, beside))
        return jnp.concatenate([piece, *came], 0), beside


def chunks_kernel(index, *refs):
    value = jnp.concatenate([ref[...] for ref in refs[:-2]], 0)
    refs[-1][...] = dot_nt(value, refs[-2][...]).astype(BF)


def chunks_product(index, value, weight_t, order, groups, name, rows_at=None):
    n = len(order)
    rows, depth = value.shape if rows_at is None else value[0].shape
    units = weight_t.shape[0]
    share = rows // groups
    specs = [pl.BlockSpec((share, depth), lambda i, index, k=k: (index[k], 0)) for k in order]
    if rows_at is not None:
        value, rows_each = value
        per = share // rows_each
        specs = [
            pl.BlockSpec((rows_each, depth), lambda i, index, k=k, b=b: (index[rows_at + per * index[k] + b], 0))
            for k in order
            for b in range(per)
        ]
    shape = (n * share, units)
    out = call(
        chunks_kernel,
        name,
        (1,),
        index,
        specs + [whole(weight_t.shape)],
        whole(shape),
        jax.ShapeDtypeStruct(shape, BF),
        [value] * len(specs) + [weight_t],
        2 * n * share * depth * units,
        32,
    )
    return out.reshape(n, share, units)


def ghid_kernel(n, begun, index, *refs):
    cots, weight, start, out = refs[:n], refs[n], refs[n + 1 : n + 1 + begun], refs[n + 1 + begun]
    for j in range(n):

        @pl.when(pl.program_id(0) == j)
        def _(j=j):
            product = dot_nt(cots[j][...], weight[...])
            if j == 0 and begun:
                out[...] = start[0][...] + product
            elif j == 0:
                out[...] = product
            else:
                out[...] += product


def ghid_product(index, members_at, cots, weight, start=()):
    keys = sorted(cots)
    n = len(keys)
    rows, depth = cots[keys[0]].shape
    units = weight.shape[0]

    def column(i, index):
        at = index[members_at + keys[0]]
        for j in range(1, n):
            at = jnp.where(i == j, index[members_at + keys[j]], at)
        return 0, at

    return call(
        functools.partial(ghid_kernel, n, len(start)),
        "head_hidden_grad",
        (n,),
        index,
        [whole((rows, depth))] * n + [pl.BlockSpec((units, depth), column)] + [whole((rows, units))] * len(start),
        whole((rows, units)),
        jax.ShapeDtypeStruct((rows, units), F32),
        [cots[k] for k in keys] + [weight, *start],
        2 * rows * units * depth * n,
        48,
    )


def down_kernel(n, index, value, weight, *refs):
    product = dot_nn(value[0], weight[...])
    if n:
        product = product + refs[0][...].astype(F32)
    refs[n][...] = product.astype(BF)


def down_product(index, side, value, weight, came=()):
    rows, units = value.shape
    half, width = rows // 2, weight.shape[1]
    return call(
        functools.partial(down_kernel, len(came)),
        "trunk_down",
        (1,),
        index,
        [
            pl.BlockSpec((1, half, units), lambda i, index: (side, 0, 0)),
            whole((units, width)),
            *[whole((half, width))] * len(came),
        ],
        whole((half, width)),
        jax.ShapeDtypeStruct((half, width), BF),
        [value.reshape(2, half, units), weight, *came],
        2 * half * units * width,
        24,
    )


def rows_kernel(index, value, out):
    out[...] = value[...]


def rows_in_order(index, rows_at, value, rows_each):
    rows, width = value.shape
    return call(
        rows_kernel,
        "rows_in_order",
        (rows // rows_each,),
        index,
        [pl.BlockSpec((rows_each, width), lambda i, index: (index[rows_at + i], 0))],
        pl.BlockSpec((rows_each, width), lambda i, index: (i, 0)),
        jax.ShapeDtypeStruct(value.shape, value.dtype),
        [value],
        rows * width,
        16,
    )


def cot_kernel(index, *refs):
    for j, ref in enumerate(refs[:-1]):

        @pl.when(pl.program_id(0) == j)
        def _(ref=ref):
            refs[-1][...] = ref[0]


def cot_columns(index, members_at, place_at, cots, rows):
    n = len(cots)
    width = cots[0].shape[1]
    mine = pl.BlockSpec((1, rows, width), lambda i, index: (index[place_at], 0, 0))
    return call(
        cot_kernel,
        "head_output_grad_rows",
        (n,),
        index,
        [mine] * n,
        pl.BlockSpec((rows, width), lambda i, index: (0, index[members_at + i])),
        jax.ShapeDtypeStruct((rows, n * width), BF),
        [cots[k].reshape(-1, rows, width) for k in range(n)],
        rows * n * width,
        32,
    )


def pre_kernel(n, begun, index, *refs):
    pieces, (gate_w, up_w), refs = refs[:n], refs[n : n + 2], refs[n + 2 :]
    start, sums, sems = refs[:begun], refs[begun : begun + 2], refs[begun + 2 :]
    copies = [pltpu.make_async_copy(start[i], sums[i], sems[0].at[i]) for i in range(begun)]
    for copy in copies:
        copy.start()
    value = jnp.concatenate([piece[...] for piece in pieces], 0)
    for i, weight in enumerate((gate_w, up_w)):
        product = dot_nt(value, weight[...])
        if begun:
            copies[i].wait()
            sums[i][...] += product
        else:
            sums[i][...] = product


def pre_product(index, offset, parts, gate_t, up_t, start=()):
    rows, depth = sum(part.shape[0] for part in parts), parts[0].shape[1]
    units = gate_t.shape[0]
    weight = pl.BlockSpec((units, depth), lambda i, index: (0, index[offset]), pipeline_mode=pl.Buffered(1))
    return call(
        functools.partial(pre_kernel, len(parts), len(start)),
        "head_pre",
        (1,),
        index,
        [whole(part.shape) for part in parts] + [weight] * 2 + [pl.BlockSpec(memory_space=pl.ANY)] * len(start),
        [whole((rows, units))] * 2,
        [jax.ShapeDtypeStruct((rows, units), F32)] * 2,
        [*parts, gate_t, up_t, *start],
        4 * rows * depth * units,
        48,
        [pltpu.SemaphoreType.DMA((2,))] if start else [],
    )


def back_rows(product, cot, own, mate):
    half = product.shape[0] // 2
    mate[0] = product[half:].astype(BF)
    mine = cot.shape[0]
    first = product[:mine] + cot[...].astype(F32)
    own[0] = jnp.concatenate([first, product[mine:half]], 0).astype(BF)


def gradients(gate, up, hidden):
    sig = jax.nn.sigmoid(gate)
    act = gate * sig
    return (hidden * up * (sig + act * (1.0 - sig))).astype(BF), (hidden * act).astype(BF)


def act_kernel(counts, places, blocks_at, index, *refs):
    n = sum(counts)
    parts, (gate_w, up_w, pre, lin, ghid, cot, dgate, dup, own, mate) = refs[:n], refs[n : n + 10]
    gate_sum, up_sum, pre_held, lin_held, ghid_held, sems = refs[n + 10 :]
    half = own.shape[1]
    copies = [pltpu.make_async_copy(pre, pre_held, sems.at[0]), pltpu.make_async_copy(lin, lin_held, sems.at[1])]
    rows_each = half // places
    for block in range(2 * places):
        into = ghid_held.at[pl.ds(block * rows_each, rows_each)]
        copies.append(pltpu.make_async_copy(ghid.at[index[blocks_at + block]], into, sems.at[2 + block]))
    for j, count in enumerate(counts):

        @pl.when(pl.program_id(0) == j)
        def _(j=j, count=count):
            if j == 0:
                for copy in copies:
                    copy.start()
            begin = sum(counts[:j])
            value = jnp.concatenate([part[...] for part in parts[begin : begin + count]], 0)
            for sums, weight in ((gate_sum, gate_w), (up_sum, up_w)):
                if j == 0:
                    sums[...] = dot_nt(value, weight[...])
                else:
                    sums[...] += dot_nt(value, weight[...])
            if j == len(counts) - 1:
                for copy in copies:
                    copy.wait()

                @pl.loop(0, 2 * half // 16)
                def _(step):
                    rows = pl.ds(pl.multiple_of(step * 16, 16), 16)
                    gate, up = gate_sum[rows] + pre_held[rows], up_sum[rows] + lin_held[rows]
                    dgate[rows], dup[rows] = gradients(gate, up, ghid_held[rows])

                product = dot_nn(dgate[...], gate_w[...]) + dot_nn(dup[...], up_w[...])
                back_rows(product, cot, own, mate)


def act_product(index, offset, pieces, gate_t, up_t, pre, lin, ghid, cot, places, blocks_at):
    flat = [part for piece in pieces for part in piece]
    depth = flat[0].shape[1]
    rows, units = pre.shape
    half = rows // 2
    last = offset + len(pieces) - 1
    weight = pl.BlockSpec((units, depth), lambda i, index: (0, index[offset + i]))
    hbm = pl.BlockSpec(memory_space=pl.ANY)
    return call(
        functools.partial(act_kernel, [len(piece) for piece in pieces], places, blocks_at),
        "head_act",
        (len(pieces),),
        index,
        [whole(part.shape) for part in flat]
        + [weight] * 2
        + [hbm] * 3
        + [pl.BlockSpec((cot.shape[0], depth), lambda i, index: (0, index[last]))],
        [whole((rows, units))] * 2 + [whole((1, half, depth))] * 2,
        [jax.ShapeDtypeStruct((rows, units), BF)] * 2 + [jax.ShapeDtypeStruct((1, half, depth), BF)] * 2,
        [*flat, gate_t, up_t, pre, lin, ghid.reshape(2 * places, half // places, units), cot],
        4 * rows * depth * units * (len(pieces) + 1),
        60,
        [pltpu.VMEM((rows, units), F32)] * 5 + [pltpu.SemaphoreType.DMA((2 + 2 * places,))],
    )


def back_kernel(index, dgate, dup, gate_w, up_w, cot, own, mate):
    product = dot_nn(dgate[...], gate_w[...]) + dot_nn(dup[...], up_w[...])
    back_rows(product, cot, own, mate)


def back_product(index, offset, count, dgate, dup, gate_t, up_t, cot, groups):
    rows, units = dgate.shape
    depth = gate_t.shape[1] // groups
    half = rows // 2
    cut = 2
    weight = pl.BlockSpec((units, depth // cut), lambda i, j, index: (0, index[offset + i] * cut + j))
    cot_spec = pl.BlockSpec((cot.shape[0], depth // cut), lambda i, j, index: (0, index[offset + i] * cut + j))
    out = pl.BlockSpec((1, half, depth // cut), lambda i, j, index: (i, 0, j))
    return call(
        back_kernel,
        "head_back",
        (count, cut),
        index,
        [whole((rows, units))] * 2 + [weight] * 2 + [cot_spec],
        [out] * 2,
        [jax.ShapeDtypeStruct((count, half, depth), BF)] * 2,
        [dgate, dup, gate_t, up_t, cot],
        4 * rows * units * depth * count,
        48,
    )


def trunk_act_kernel(groups, index, *refs):
    ghids, gates, ups = refs[: 2 * groups], refs[2 * groups : 3 * groups], refs[3 * groups : 4 * groups]
    gate_w, up_w, dgate, dup, own, mate = refs[4 * groups :]
    for k in range(groups):
        share = gates[k].shape[0]
        for side in range(2):
            part = share // 2
            tile = 16 if part % 16 == 0 else part

            @pl.loop(0, part // tile)
            def _(step, k=k, side=side, part=part, tile=tile):
                at = pl.multiple_of(step * tile, tile)
                ghid = ghids[2 * k + side][pl.ds(at, tile)].astype(F32)
                rows = pl.ds(pl.multiple_of(side * part + at, tile), tile)
                gate, up = gates[k][rows].astype(F32), ups[k][rows].astype(F32)
                rows = pl.ds(pl.multiple_of(index[k] * share + side * part + at, tile), tile)
                dgate[rows], dup[rows] = gradients(gate, up, ghid)

    half = own.shape[0]
    for side, out in enumerate((own, mate)):
        rows = slice(side * half, side * half + half)
        product = dot_nn(dgate[rows], gate_w[...]) + dot_nn(dup[rows], up_w[...])
        out[...] = product.astype(BF)


def trunk_act(index, ghids, gates, ups, gate_t, up_t):
    groups = len(gates)
    share, units = gates[0].shape
    rows, width = share * groups, gate_t.shape[1]
    flat = [half for pair in ghids for half in pair]
    shapes = [(rows, units)] * 2 + [(rows // 2, width)] * 2
    return call(
        functools.partial(trunk_act_kernel, groups),
        "trunk_act",
        (1,),
        index,
        [whole(v.shape) for v in [*flat, *gates, *ups, gate_t, up_t]],
        [whole(shape) for shape in shapes],
        [jax.ShapeDtypeStruct(shape, BF) for shape in shapes],
        [*flat, *gates, *ups, gate_t, up_t],
        4 * rows * units * width,
        36,
    )


def grads_kernel(index, dgate, dup, toks, gate, up):
    gate[...] = dot(dgate[...], toks[...], ((0,), (0,)))
    up[...] = dot(dup[...], toks[...], ((0,), (0,)))


def grads_product(index, dgate, dup, toks):
    rows, units = dgate.shape
    width = toks.shape[1]
    tile = width // 2
    out = pl.BlockSpec((units, tile), lambda i, index: (0, i))
    return call(
        grads_kernel,
        "trunk_weight_grads",
        (2,),
        index,
        [whole((rows, units))] * 2 + [pl.BlockSpec((rows, tile), lambda i, index: (0, i))],
        [out] * 2,
        [jax.ShapeDtypeStruct((units, width), F32)] * 2,
        [dgate, dup, toks],
        4 * rows * units * width,
        48,
    )


def make_body(plan):
    groups, places = plan.groups, plan.places

    def body(tokens, trunk_gate, trunk_up, trunk_down, head_gate, head_up, head_down, head_grads):
        g = lax.axis_index("group")
        m = lax.axis_index("mp")
        z, c = m // 2, m % 2
        total_rows, width = tokens.shape
        rows = total_rows // plan.members
        units = trunk_gate.shape[1]
        half_rows = places * rows
        share = total_rows // groups
        offsets = [g ^ k for k in range(groups)]
        both = [(k, side) for side in range(2) for k in range(places)]
        blocks = [(c ^ side) * places + (z ^ k) for k, side in both]
        members = [2 * (z ^ k) + (c ^ side) for k in range(places) for side in range(2)]
        blocks_at, members_at = groups, groups + plan.members
        rows_at = members_at + plan.members
        index = jnp.stack(offsets + blocks + members + [2 * (z ^ k) + (c ^ side) for k, side in both]).astype(jnp.int32)

        own_tok = row(tokens.reshape(plan.members, rows, width), m)
        cot_width = head_grads.shape[2]
        cot_own = head_grads[0].reshape(places, 2, rows, cot_width).transpose(1, 0, 2, 3)
        cot_own = cot_own.reshape(total_rows, cot_width)

        def in_order(pieces):
            out = jnp.zeros((groups, 2, share // 2, units), BF)
            for k, pair in pieces.items():
                if isinstance(pair, tuple):
                    for side in range(2):
                        out = lax.dynamic_update_slice(out, pair[side][None, None], (g ^ k, side, 0, 0))
                else:
                    out = lax.dynamic_update_slice(out, pair[None], (g ^ k, 0, 0, 0))
            return out.reshape(total_rows, units)

        def sums(weight, first, name):
            keep = [k for k in range(groups) if not k & first]
            send = [k for k in range(groups) if k & first]
            sent = chunks_product(index, (tokens, rows), weight.T, send, groups, name, rows_at)
            return sent, lambda: chunks_product(index, (tokens, rows), weight.T, keep, groups, name, rows_at)

        gate_send, gate_keep = sums(trunk_gate, 1, "trunk_gate")
        up_send, up_keep = sums(trunk_up, 2, "trunk_up")
        gate_came, up_came = plan.group_swap(gate_send, 1), plan.group_swap(up_send, 2)
        gate_kept, up_kept = gate_keep(), up_keep()
        near = [k for k in range(1, places) if not k & (k - 1)][::-1]
        far = [k for k in range(1, places) if k & (k - 1)]
        crossed = {k: plan.place_swap(cot_own, k) for k in near}
        cots = {0: cot_own, 1: plan.core_swap(cot_own)}
        ghid = ghid_product(index, members_at, cots, head_down[0])
        toks = rows_in_order(index, rows_at, tokens, rows)
        gate_came, up_came, ghid, toks = tie(gate_came, up_came, ghid, toks)
        gate_r = plan.halving(gate_kept, gate_came, 1)
        up_r = plan.halving(up_kept, up_came, 2)
        gate_r, up_r, crossed = lax.optimization_barrier((gate_r, up_r, crossed))

        def both_members(which):
            pairs = [((2 * k, crossed[k]), (2 * k + 1, plan.core_swap(crossed[k]))) for k in which]
            return dict(sum(pairs, ()))

        came_first, came_next = both_members(near[:1]), both_members(near[1:])
        for k in far:
            crossed[k] = plan.place_swap(crossed[k & (k - 1)], k & -k)
        hid_r = (jax.nn.silu(gate_r) * up_r).astype(BF)
        wide, (ghid, came_next, got) = plan.gather(
            hid_r.reshape(2, share // 2, units),
            second=lambda have, done: (
                ghid_product(index, members_at, came_first, head_down[0], (ghid,)),
                came_next,
                [crossed[k] for k in far],
            ),
        )
        crossed |= dict(zip(far, got))
        hidden = in_order(wide)
        pair = jnp.stack([gate_r, up_r]).astype(BF)
        hidden, pair = tie(hidden, pair)
        have = plan.hop_one(pair)
        came = plan.core_swap(down_product(index, 1, hidden, trunk_down))
        part = down_product(index, 0, hidden, trunk_down, (came,))
        came_last = came_next | both_members(far)
        part, came_last = lax.optimization_barrier((part, came_last))
        ghid = ghid_product(index, members_at, came_last, head_down[0], (ghid,))
        beside = (ghid, have)
        summed, (ghid, have) = plan.place_sum(part.reshape(places, rows, width), beside)
        cots |= came_first | came_last
        shard = (own_tok.astype(F32) + summed).astype(BF)
        shard, have, cots = lax.optimization_barrier((shard, have, cots))
        gate_t, up_t = head_gate[0].T, head_up[0].T
        cot_rows = cot_columns(index, members_at, blocks_at, cots, rows)
        came = {k: plan.place_swap(shard, k) for k in range(1, places)}
        inner = places // 2
        near, have = lax.optimization_barrier(({k: came[k] for k in range(1, inner)}, have))
        top = jnp.concatenate([shard] + [near[k] for k in range(1, inner)], 0)
        wide = [plan.hop_one(top), None]
        rest = plan.hop_two(have)
        far, wide[0], cot_rows = lax.optimization_barrier(
            ({k: came[k] for k in range(inner, places)}, wide[0], cot_rows)
        )
        low = jnp.concatenate([far[k] for k in range(inner, places)], 0)
        wide[1] = plan.hop_one(low)
        relayed = [plan.group_swap(wide[0][2], 1)] if groups == 4 else []

        def both_cores(parts):
            return parts + [plan.core_swap(part) for part in parts]

        pre, lin = pre_product(index, 0, both_cores([top, low]), gate_t, up_t)
        wide, rest, relayed, pre, lin = lax.optimization_barrier((wide, rest, relayed, pre, lin))
        have = have | rest
        gates, ups = ([have[k][i] for k in range(groups)] for i in range(2))
        relayed += [plan.group_swap(wide[1][1], 2)] if groups == 4 else []
        pieces = [both_cores([half[k] for half in wide]) for k in range(2, groups) if k in wide[0]]
        pre, lin = pre_product(index, 1, both_cores([half[1] for half in wide]), gate_t, up_t, (pre, lin))
        relayed, pieces, pre, lin = lax.optimization_barrier((relayed, pieces, pre, lin))
        pieces += [both_cores(relayed)] if groups == 4 else []
        dgate, dup, *last_block = act_product(
            index, 2, pieces, gate_t, up_t, pre, lin, ghid, cot_rows, places, blocks_at
        )

        def make(offset, count, hops, hold):
            if groups == 4 and offset == groups - 1:
                own, mate = last_block
            else:
                own, mate = back_product(index, offset, count, *hold, gate_t, up_t, cot_rows, groups)
            if hops is not None:
                if offset:
                    own, mate, hops = lax.optimization_barrier((own, mate, hops))
                else:
                    own, hops = lax.optimization_barrier((own, hops))
            total = own.astype(F32) + plan.core_swap(mate).astype(F32)
            parts = {offset + i: total[i].reshape(2, half_rows // 2, width) for i in range(count)}
            return parts if hops is None else (parts, hops)

        cols = plan.scatter(make, (dgate, dup))
        dshard = plan.place_sum(cols.astype(BF).reshape(places, rows, width))[0].astype(BF)
        dhalf = plan.place_gather(dshard)[0]
        grad_mid = jnp.concatenate([dhalf, plan.core_swap(dhalf)], 0)

        back = chunks_product(index, grad_mid, trunk_down, list(range(groups)), groups, "trunk_hidden_grad")
        back = back.reshape(groups, 2, share // 2, units)

        def chunks(offset, count, hops, hold):
            parts = {offset + i: back[offset + i] for i in range(count)}
            return parts if hops is None else (parts, hops)

        ghid_t = plan.scatter(chunks, ()).astype(BF)
        wide, (grad_down,) = plan.gather(ghid_t, lambda: (dot(hidden, grad_mid, ((0,), (0,))),))
        ghids = [wide[k] for k in range(groups)]
        dgate_t, dup_t, own, mate = trunk_act(index, ghids, gates, ups, trunk_gate.T, trunk_up.T)
        part = (own.astype(F32) + plan.core_swap(mate).astype(F32)).astype(BF)
        part, dgate_t, dup_t = tie(part, dgate_t, dup_t)
        grads = grads_product(index, dgate_t, dup_t, toks)
        summed, (grad_gate, grad_up) = plan.place_sum(part.reshape(places, rows, width), grads)
        grad_x = (dshard.astype(F32) + summed).astype(BF)
        grad_gate, grad_up = grad_gate.T, grad_up.T
        return (grad_x, grad_gate, grad_up, grad_down)

    return body


def solution(mesh):
    return jax.shard_map(
        make_body(Plan(mesh)),
        mesh=mesh,
        in_specs=(
            P(None, "group"),
            P("group", "mp"),
            P("group", "mp"),
            P("mp", "group"),
            P("group", None, "mp"),
            P("group", None, "mp"),
            P("group", "mp", None),
            P("group", None, "mp"),
        ),
        out_specs=(P("mp", "group"), P("group", "mp"), P("group", "mp"), P("mp", "group")),
        check_vma=False,
    )
```
